512 devices in a mesh: ctx: 64 (over z, y), head: 8 (over x, core).
Axes of the slice: x: 4, y: 8, z: 8, core: 2. Of those that a mesh axis runs over, the one named last changes fastest.
Arguments:
- tokens: bfloat16 [8192, 2048], P('ctx'), may hold values from -6 to 6
- w_query: bfloat16 [2048, 1024], P('ctx', 'head'), may hold values from -0.125 to 0.125
- w_key: bfloat16 [2048, 1024], P('ctx', 'head'), may hold values from -0.125 to 0.125
- w_value: bfloat16 [2048, 2048], P('ctx', 'head'), may hold values from -0.125 to 0.125
- w_output_gate: bfloat16 [2048, 2048], P('ctx', 'head'), may hold values from -0.125 to 0.125
- w_beta: bfloat16 [2048, 16], P('ctx', 'head'), may hold values from -0.125 to 0.125
- w_decay: bfloat16 [2048, 16], P('ctx', 'head'), may hold values from -0.125 to 0.125
- decay_rate: float32 [16], P('head'), may hold values from 0.00024414062 to 0.04
- dt_bias: float32 [16], P('head'), may hold values from -3 to 3
- conv_qk: float32 [4, 2, 1024], P(None, None, 'head'), may hold values from -3 to 3
- conv_value: float32 [4, 2048], P(None, 'head'), may hold values from -3 to 3
- norm_gain: float32 [128], replicated, may hold values from 0.1 to 1.9
- w_out: bfloat16 [2048, 2048], P('head'), may hold values from -0.1875 to 0.1875
- doc_lengths: int32 [32], replicated, may hold values from 1 to 2048, 8192 in all
Outputs:
- mixed: bfloat16 [8192, 2048], P('ctx', 'head')
The draws below stay inside these ranges and needn't reach their ends.
Inputs may be any that keep to these rules, and one draw needn't show every extreme that they name: `doc_lengths`: the 32 documents lie end to end in this order and cover all 8192 tokens; the longest has exactly 2048 tokens.
All inputs are finite; a program needn't handle non-finite values.
Results may differ from the reference program's by a relative error of at most 0.013.
Values may be sent and summed in bfloat16 or wider, within the bound.
A program may use at most 64 MiB of HBM per device.

```python
import math
import jax
import jax.numpy as jnp
import numpy as np
from jax import lax

D = 2048
NK = 8
NH = 16
HEAD_DIM = 128
SPAN = 64
KERNEL = 4
DOCS = 32
TOKENS = 8192
DOC_MOST = 2048


def spiked(entries, stream_key, source, target, shards_of, factor):
    def block_of(dim):
        return (jnp.arange(entries.shape[dim]) // (entries.shape[dim] // shards_of)).reshape((-1,) + (1,) * (entries.ndim - 1 - dim))

    one_side = jax.random.permutation(stream_key, shards_of)[block_of(target)]
    far = (block_of(target) + shards_of // 2) % shards_of
    return jnp.where((block_of(source) == one_side) | (block_of(source) == far), factor * entries, entries)


def block_levels(own_key, shape, split, low, high):
    level, own = 1.0, jax.random.fold_in(own_key, 6)
    for position, blocks in split:
        draws = jnp.exp(jax.random.uniform(jax.random.fold_in(own, position), (blocks,), jnp.float32, low / len(split), high / len(split)))
        level = level * jnp.repeat(draws, shape[position] // blocks).reshape([-1 if axis == position else 1 for axis in range(len(shape))])
    return level


def length_profile(number_of, total, reach, slope):
    loads = [(1 << 20) // math.isqrt(grade ** slope) + 1 for grade in range(2, number_of + 1)]
    rest, holding = total - reach - (number_of - 1), [1] * (number_of - 1)
    while rest > 0:
        movable = [i for i in range(number_of - 1) if holding[i] < reach]
        pool, budget = sum([loads[i] for i in movable]), rest
        for i in movable:
            extra = min(reach - holding[i], max(1, budget * loads[i] // pool), rest)
            holding[i] = holding[i] + extra
            rest = rest - extra
    return np.array([reach] + holding)


def ragged(rng, number_of, total, reach, slope):
    if number_of == 2:
        one = jax.random.randint(rng, (), max(1, total - reach), min(reach, total - 1) + 1)
        return jnp.stack([one, total - one])
    lengths = jnp.asarray(length_profile(number_of, total, reach, slope), jnp.int32)
    couples = (number_of - 1) // 2
    donor, receiver = lengths[1:1 + 2 * couples:2], lengths[2:2 + 2 * couples:2]
    slack = jnp.minimum(donor - 1, reach - receiver)
    moved = jax.random.randint(jax.random.fold_in(rng, 1), (couples,), 0, 1 << 20) % (slack + 1)
    lengths = lengths.at[1:1 + 2 * couples:2].set(donor - moved).at[2:2 + 2 * couples:2].set(receiver + moved)
    return lengths[jax.random.permutation(jax.random.fold_in(rng, 2), number_of)]


def gaussian(key, extent, deviation, most, split=(), kind=jnp.bfloat16):
    entries = deviation * jax.random.normal(key, extent, jnp.float32)
    if split:
        entries = entries * block_levels(key, extent, split, -0.22, 0.18)
    return jnp.clip(entries, -most, most).astype(kind)


def heavy_noise(stream_key, extent, spread, bound, pieces, heavy, kind=jnp.bfloat16):
    values = spread * jax.random.normal(stream_key, extent, jnp.float32)
    if pieces:
        values = values * block_levels(stream_key, extent, pieces, -0.22, 0.18)
    return jnp.clip(spiked(values, jax.random.fold_in(stream_key, 3), *heavy), -bound, bound).astype(kind)


def setup_inputs(seed: int = 0) -> dict:
    arg_keys = jax.random.split(jax.random.key(seed), 15)
    tokens = gaussian(arg_keys[0], (TOKENS, D), 1.0, 6.0, ((0, 64),))
    w_query = gaussian(arg_keys[1], (D, NK * HEAD_DIM), D ** -0.5, 0.125, ((0, 64), (1, 8)))
    w_key = gaussian(arg_keys[2], (D, NK * HEAD_DIM), D ** -0.5, 0.125, ((0, 64), (1, 8)))
    w_value = gaussian(arg_keys[3], (D, NH * HEAD_DIM), D ** -0.5, 0.125, ((0, 64), (1, 8)))
    w_output_gate = gaussian(arg_keys[4], (D, NH * HEAD_DIM), D ** -0.5, 0.125, ((0, 64), (1, 8)))
    w_beta = gaussian(arg_keys[5], (D, NH), D ** -0.5, 0.125, ((0, 64), (1, 8)))
    w_decay = gaussian(arg_keys[6], (D, NH), D ** -0.5, 0.125, ((0, 64), (1, 8)))
    decay_rate = jnp.clip(jnp.exp(math.log(0.04) - 5.0988903 * jax.random.uniform(arg_keys[7], (NH,), jnp.float32) ** block_levels(arg_keys[7], (NH,), ((0, 8),), -0.2, 0.2)), 0.00024414062, 0.04)
    dt_bias = jnp.clip(jax.random.uniform(arg_keys[8], (NH,), jnp.float32, -3.0, 3.0) * block_levels(arg_keys[8], (NH,), ((0, 8),), -0.4, 0.0), -3.0, 3.0)
    conv_qk = gaussian(arg_keys[9], (KERNEL, 2, NK * HEAD_DIM), 0.5, 3.0, ((2, 8),), jnp.float32)
    conv_value = gaussian(arg_keys[10], (KERNEL, NH * HEAD_DIM), 0.5, 3.0, ((1, 8),), jnp.float32)
    norm_gain = jnp.clip(1.0 + 0.18 * jax.random.normal(arg_keys[11], (HEAD_DIM,), jnp.float32), 0.1, 1.9)
    w_out = heavy_noise(arg_keys[12], (NH * HEAD_DIM, D), (NH * HEAD_DIM) ** -0.5, 0.1875, ((0, 8),), (0, 1, 8, 2.0))
    doc_lengths = ragged(arg_keys[13], DOCS, TOKENS, DOC_MOST, 2).astype(jnp.int32)
    return {"tokens": tokens, "w_query": w_query, "w_key": w_key, "w_value": w_value, "w_output_gate": w_output_gate, "w_beta": w_beta, "w_decay": w_decay, "decay_rate": decay_rate, "dt_bias": dt_bias, "conv_qk": conv_qk, "conv_value": conv_value, "norm_gain": norm_gain, "w_out": w_out, "doc_lengths": doc_lengths}


HIGH = lax.Precision.HIGHEST
EPSILON = 1e-06

def segment_of(offsets, positions):
    return lax.optimization_barrier(jnp.sum((offsets[None, :] <= positions[:, None]).astype(jnp.int32), axis=1))

def short_conv(extended, seg_ext, kernel, length):
    width = kernel.shape[0]
    total = jnp.zeros((length, extended.shape[1]), extended.dtype)
    for tap_index in range(width):
        keep = seg_ext[tap_index:tap_index + length] == seg_ext[width - 1:]
        total = total + jnp.where(keep[:, None], extended[tap_index:tap_index + length], 0.0) * kernel[tap_index]
    return jax.nn.silu(total)

def head_inputs(mixed_act, key_heads, beta_logit, decay_logit, decay_rate, dt_bias):
    length = mixed_act.shape[0]
    heads = beta_logit.shape[1]
    inner = key_heads * HEAD_DIM
    queries = mixed_act[:, :inner].reshape(length, key_heads, HEAD_DIM)
    keyed = mixed_act[:, inner:2 * inner].reshape(length, key_heads, HEAD_DIM)
    values = mixed_act[:, 2 * inner:].reshape(length, heads, HEAD_DIM)
    queries = queries * lax.rsqrt(lax.optimization_barrier(jnp.sum(queries * queries, axis=2, keepdims=True)) + EPSILON) * HEAD_DIM ** (-0.5)
    keyed = keyed * lax.rsqrt(lax.optimization_barrier(jnp.sum(keyed * keyed, axis=2, keepdims=True)) + EPSILON)
    group = heads // key_heads
    queries = jnp.repeat(queries, group, axis=1)
    keyed = jnp.repeat(keyed, group, axis=1)
    beta = jax.nn.sigmoid(beta_logit)
    decay = -decay_rate * jax.nn.softplus(decay_logit + dt_bias)
    return (queries, keyed, values, beta, decay)

def to_blocks(array):
    length = array.shape[0]
    shaped = array.reshape((length // SPAN, SPAN) + array.shape[1:])
    if array.ndim == 3:
        return shaped.transpose(0, 2, 1, 3)
    return shaped.transpose(0, 2, 1)

def unit_lower_inverse(lower):
    size = lower.shape[-1]
    identity = jnp.eye(size, dtype=lower.dtype)
    inverse = identity - lower
    power = lower
    for level in range(size.bit_length() - 2):
        power = jnp.einsum('hij,hjk->hik', power, power, precision=HIGH)
        inverse = jnp.einsum('hij,hjk->hik', inverse, identity + power, precision=HIGH)
    return inverse

def span_factors(keyed, values, beta, decay, seg, prev_seg):
    size = seg.shape[0]
    gam = jnp.cumsum(decay, axis=1)
    order = jnp.arange(size, dtype=jnp.int32)
    same = (seg[:, None] == seg[None, :]) & (order[:, None] >= order[None, :])
    diff = jnp.where(same[None], gam[:, :, None] - gam[:, None, :], 0.0)
    ratio = jnp.where(same[None], jnp.exp(diff), 0.0)
    lead = jnp.where((seg == prev_seg)[None], jnp.exp(gam), 0.0)
    inner = jnp.einsum('hid,hjd->hij', keyed, keyed, precision=HIGH)
    strict = order[:, None] > order[None, :]
    lower = jnp.where(strict[None], beta[:, :, None] * ratio * inner, 0.0)
    inverse = unit_lower_inverse(lower)
    right = jnp.concatenate([beta[..., None] * values, (beta * lead)[..., None] * keyed], axis=2)
    solved = jnp.einsum('hij,hjd->hid', inverse, right, precision=HIGH)
    return (solved[..., :HEAD_DIM], solved[..., HEAD_DIM:], ratio, lead)

def span_run(state, queries, keyed, update, writer, ratio, lead):
    fresh = update - jnp.einsum('hcd,hed->hce', writer, state, precision=HIGH)
    scores = jnp.einsum('hid,hjd->hij', queries, keyed, precision=HIGH) * ratio
    carried = jnp.einsum('hcd,hed->hce', queries, state, precision=HIGH)
    result = lead[..., None] * carried + jnp.einsum('hij,hje->hie', scores, fresh, precision=HIGH)
    tail = ratio[:, -1, :]
    new_state = lead[:, -1][:, None, None] * state + jnp.einsum('hje,hjd->hed', fresh, tail[..., None] * keyed, precision=HIGH)
    return (new_state, result)

def gated_norm(result, gate_proj, norm_gain):
    length, heads = (result.shape[0], result.shape[1])
    scaled = result * lax.rsqrt(lax.optimization_barrier(jnp.mean(result * result, axis=2, keepdims=True)) + EPSILON) * norm_gain
    gate = gate_proj.astype(jnp.float32).reshape(length, heads, HEAD_DIM)
    return (scaled * jax.nn.silu(gate)).reshape(length, heads * HEAD_DIM).astype(jnp.bfloat16)

def reference(tokens, w_query, w_key, w_value, w_output_gate, w_beta, w_decay, decay_rate, dt_bias, conv_qk, conv_value, norm_gain, w_out, doc_lengths):

    def project(weight):
        return jnp.dot(tokens, weight, preferred_element_type=jnp.float32)
    query_proj = project(w_query).astype(jnp.bfloat16)
    key_proj = project(w_key).astype(jnp.bfloat16)
    value_proj = project(w_value).astype(jnp.bfloat16)
    gate_proj = project(w_output_gate).astype(jnp.bfloat16)
    beta_logit = project(w_beta)
    decay_logit = project(w_decay)
    offsets = (jnp.cumsum(doc_lengths) - doc_lengths).astype(jnp.int32)
    positions = jnp.arange(-(KERNEL - 1), TOKENS, dtype=jnp.int32)
    seg_ext = segment_of(offsets, positions)
    joined = jnp.concatenate([query_proj, key_proj, value_proj], axis=1)
    padding = jnp.zeros((KERNEL - 1, joined.shape[1]), joined.dtype)
    extended = jnp.concatenate([padding, joined], axis=0).astype(jnp.float32)
    kernel = jnp.concatenate([conv_qk.reshape(KERNEL, -1), conv_value], axis=1)
    mixed_act = short_conv(extended, seg_ext, kernel, TOKENS)
    queries, keyed, values, beta, decay = head_inputs(mixed_act, NK, beta_logit, decay_logit, decay_rate, dt_bias)
    token_seg = seg_ext[KERNEL - 1:].reshape(TOKENS // SPAN, SPAN)
    prev_seg = seg_ext[KERNEL - 2:KERNEL - 2 + TOKENS:SPAN]

    def advance(state, items):
        query_c, key_c, value_c, beta_c, decay_c, seg_c, prev_c = items
        update, writer, ratio, lead = span_factors(key_c, value_c, beta_c, decay_c, seg_c, prev_c)
        return span_run(state, query_c, key_c, update, writer, ratio, lead)
    start = jnp.zeros((NH, HEAD_DIM, HEAD_DIM), jnp.float32)
    items = (to_blocks(queries), to_blocks(keyed), to_blocks(values), to_blocks(beta), to_blocks(decay), token_seg, prev_seg)
    final, outputs = lax.scan(advance, start, items)
    result = outputs.transpose(0, 2, 1, 3).reshape(TOKENS, NH, HEAD_DIM)
    normed = gated_norm(result, gate_proj, norm_gain)
    return jnp.dot(normed, w_out, preferred_element_type=jnp.float32).astype(jnp.bfloat16)
```

```python
import jax
import jax.numpy as jnp
from jax import lax
from jax.experimental import pallas as pl
from jax.experimental.pallas import tpu as pltpu
from jax.sharding import PartitionSpec as P

MESH = pl.DeviceIdType.MESH
HIGH = lax.Precision.HIGHEST
EPSILON = 1e-06
HD = 128
BLOCK = 128
RIM = 16
F32 = jnp.float32
BF16 = jnp.bfloat16
FAR = 1 << 20


def dot(a, b, dims=((1,), (0,)), precision=HIGH):
    return lax.dot_general(a, b, (dims, ((), ())), precision=precision, preferred_element_type=F32)


def iota(shape, dim):
    return lax.broadcasted_iota(jnp.int32, shape, dim)


def unit_lower_inverse(lower):
    size = lower.shape[0]
    row, col = iota(lower.shape, 0), iota(lower.shape, 1)
    inverse = jnp.where(row == col, 1.0, 0.0)
    shift = 0
    while (1 << shift) < size:
        joins = ((row >> (shift + 1)) == (col >> (shift + 1))) & ((row >> shift) != (col >> shift))
        part = jnp.where(joins, lower, 0.0)
        if shift == 0:
            inverse = inverse - part
        else:
            inverse = inverse - dot(dot(inverse, part), inverse)
        shift += 1
    return inverse


def block_state(k, v, beta, g, start):
    row, col = iota((BLOCK, BLOCK), 0), iota((BLOCK, BLOCK), 1)
    lower_tri = row >= col
    gam = dot(jnp.where(lower_tri, 1.0, 0.0), g)
    same = lower_tri & (col >= start)
    ratio = jnp.where(same, jnp.exp(jnp.where(same, gam - gam.T, 0.0)), 0.0)
    lead = jnp.where(start < 0, jnp.exp(gam), 0.0)
    inner = dot(k, k, ((1,), (1,)))
    inverse = unit_lower_inverse(jnp.where(row > col, beta * ratio * inner, 0.0))
    solved = dot(inverse, jnp.concatenate([beta * v, beta * lead * k], axis=1))
    tail = jnp.where(row >= start[BLOCK - 1 :], jnp.exp(gam[BLOCK - 1 :] - gam), 0.0)
    joint = dot(solved, tail * k, ((0,), (0,)))
    transition = jnp.where(row == col, lead[BLOCK - 1 :], 0.0) - joint[HD:]
    return jnp.concatenate([joint[:HD], transition], axis=0), solved, ratio, lead


def block_output(q, k, solved, ratio, lead):
    scores = dot(q, k, ((1,), (1,))) * ratio
    mixed = dot(scores, solved)
    return lead * q - mixed[:, HD:], mixed[:, :HD]


def compose(earlier, later):
    joined = dot(earlier, later[HD:])
    return jnp.concatenate([joined[:HD] + later[:HD], joined[HD:]], axis=0)


def sigmoid(x):
    return 1.0 / (1.0 + jnp.exp(-x))


def kernel(
    tokens, w_query, w_key, w_value, w_gate, w_beta, w_decay, rate, bias, conv_qk, conv_value, gain, w_out, docs,
    out,
    x_all, w_mine, w_other, wo_all, w_stage, piece, pieces, p_mine, p_other, acc, logit,
    z_unit, z_first, z_send, z_in, s_in, n_stage, n_all,
    send_sem, a1_sem, a2_sem, rim_sem, y_sem, p_sem, z_sem, c_sem, wo_sem, par_sem, zf_sem, zi_sem, si_sem, n_sem, own_sem,
):
    ctx, head = lax.axis_index("ctx"), lax.axis_index("head")
    z, y = ctx // 8, ctx % 8
    x, c = head // 2, head % 2
    group, yl, yh = ctx // 4, ctx % 4, (ctx % 8) // 4
    hl = jnp.where(yh == 0, y, 7 - y)
    partner = (ctx, 2 * x + 1 - c)

    def place(g, local):
        g = lax.rem(g + 16, 16)
        return 8 * (g // 2) + jnp.where(g % 2 == 0, local, 7 - local)

    pending = []

    def send(src, dst, recv, device, cond=None):
        copy = pltpu.make_async_remote_copy(
            src_ref=src, dst_ref=dst, send_sem=send_sem.at[len(pending)], recv_sem=recv,
            device_id=device, device_id_type=MESH,
        )
        if cond is None:
            copy.start()
        else:
            pl.when(cond)(copy.start)
        pending.append((copy, cond))

    def arrived(dst, sem):
        pltpu.make_async_copy(dst, dst, sem).wait()

    barrier = pltpu.get_barrier_semaphore()

    def greet(device):
        pl.semaphore_signal(barrier, inc=1, device_id=device, device_id_type=MESH)

    for i in range(1, 8):
        other = 8 * z + lax.rem(y + i, 8)
        greet((other, 2 * x))
        greet((other, 2 * x + 1))
    for i in range(1, 8):
        greet((ctx, lax.rem(head + i, 8)))
    greet((lax.rem(ctx + 8, 64), head))
    greet((lax.rem(ctx + 56, 64), head))
    pl.when((c == 0) & (yh == 0))(lambda: greet((lax.rem(4 * group + 63, 64), 2 * x + 1)))

    @pl.when(c == 1)
    def _():
        for d in range(1, 5):
            greet((place(group - d, hl), head))

    rim_across = (c == 1) & (y == 7)

    for s in range(4):
        for i in range(2):
            p_mine[2 * s + i : 2 * s + i + 1, :] = conv_qk[s, i : i + 1, :]
        for i in range(2):
            p_mine[8 + 4 * i + s : 9 + 4 * i + s, :] = conv_value[s : s + 1, HD * i : HD * i + HD]
    for i in range(2):
        p_mine[16 + 2 * i : 17 + 2 * i, :] = jnp.full((1, HD), rate[i], F32)
        p_mine[17 + 2 * i : 18 + 2 * i, :] = jnp.full((1, HD), bias[i], F32)
    w_stage[0, :, :HD] = w_query[...]
    w_stage[0, :, HD:] = w_key[...]
    for i in range(2):
        w_stage[1 + i, :, :HD] = w_value[:, HD * i : HD * i + HD]
        w_stage[1 + i, :, HD:] = w_gate[:, HD * i : HD * i + HD]
    spot = iota((32, HD), 1) == iota((32, HD), 0) + 32 * (y % 4)
    total = jnp.zeros((16, HD), F32)
    for i, column in enumerate(
        (w_beta[:, 0:1], w_beta[:, 1:2], w_decay[:, 0:1], w_decay[:, 1:2])
    ):
        line = jnp.sum(jnp.where(spot, column.astype(F32), 0.0), axis=0, keepdims=True)
        total = jnp.where(iota((16, HD), 0) == i, line, total)
    piece[...] = total.astype(BF16)

    pl.semaphore_wait(barrier, 23 + 4 * c + 4 * rim_across.astype(jnp.int32))

    mine_rows = pl.ds(pl.multiple_of(32 * y, 32), 32)
    selfs = []
    for sub in range(2):
        local = 2 * c + sub
        for half in range(2):
            to = 8 * z + (local if half == 0 else 7 - local)
            me = to == ctx
            for core in range(2):
                device = (to, 2 * x + core)
                src = w_stage.at[0] if core == 0 else w_stage.at[1 + sub]
                is_self = me & (c == core)
                dst = w_mine.at[z, mine_rows, :]
                send(src, dst, y_sem.at[y], device, ~is_self)
                send(piece, pieces.at[y], p_sem.at[y], device, ~is_self)
                selfs.append((src, dst, is_self))
    for src, dst, is_self in selfs:

        @pl.when(is_self)
        def _(src=src, dst=dst):
            pltpu.make_async_copy(src, dst, y_sem.at[y]).start()
            pltpu.make_async_copy(piece, pieces.at[y], p_sem.at[y]).start()

    quarter = pl.ds(pl.multiple_of(32 * x, 32), 32)
    owner = yl // 2 == c
    for i in range(1, 4):
        to = 4 * group + lax.rem(yl + i, 4)
        rows = pl.ds(pl.multiple_of(RIM + 128 * (yl % 2) + 32 * x, 16), 32)
        send(tokens.at[quarter, :], x_all.at[rows, :], a1_sem.at[yl % 2], (to, head), owner)
    after_two = (c == 0) & (yl == 1)
    after_four = (c == 1) & (yl == 3)
    for i in range(4):
        last = tokens.at[pl.ds(128 - RIM, RIM), :]
        to = jnp.where(after_two, 4 * group + i, lax.rem(4 * group + 4 + i, 64))
        send(last, x_all.at[pl.ds(0, RIM), :], rim_sem, (to, 2 * x + 1 - c), after_two | after_four)
    send(p_mine, p_other, par_sem, partner)
    own_block = []
    for k in range(2):
        is_own = yl == 2 * c + k
        block = x_all.at[pl.ds(RIM + 128 * k, 128), :]
        own_block.append((is_own, pltpu.make_async_copy(tokens, block, own_sem.at[0])))
        pl.when(is_own)(own_block[-1][1].start)
    own_out = pltpu.make_async_copy(
        w_out.at[:, pl.ds(pl.multiple_of(256 * head, 256), 256)],
        wo_all.at[pl.ds(pl.multiple_of(256 * head, 256), 256), :],
        own_sem.at[1],
    )
    own_out.start()

    base = 512 * group + 256 * c
    place_of = iota((256, HD), 0)
    start = jnp.full((256, HD), -FAR, jnp.int32)
    offset = -base
    for i in range(32):
        start = jnp.maximum(start, jnp.where(place_of >= offset, offset, -FAR))
        offset = offset + docs[i]

    for i in range(8):
        arrived(w_mine.at[z, pl.ds(32 * i, 32), :], y_sem.at[i])
        arrived(pieces.at[i], p_sem.at[i])
    for i in range(2):
        joined = sum(pieces[4 * i + j].astype(F32) for j in range(4))
        w_mine[z, 256:272, HD * i : HD * i + HD] = joined.astype(BF16)

    ups, downs = lax.rem(ctx + 8, 64), lax.rem(ctx + 56, 64)
    chunks = (pl.ds(0, 144), pl.ds(144, 128))
    cores = (pl.ds(0, 144), pl.ds(144, 112))

    def onward(bundle, step, way, part):
        ref = w_mine.at[bundle, chunks[part], :]
        send(ref, ref, z_sem.at[way, step - 1, part], (ups if way == 0 else downs, head))

    def across(bundle, part):
        send(w_mine.at[bundle, cores[part], :], w_other.at[bundle, cores[part], :], c_sem.at[bundle, part], partner)

    for part in range(2):
        onward(z, 1, 0, part)
        onward(z, 1, 1, part)
    for part in range(2):
        across(z, part)

    for k in range(2):
        is_remote = yl != 2 * c + k
        rows = pl.ds(pl.multiple_of(RIM + 128 * k + 32 * x, 16), 32)
        pl.when(is_remote)(lambda rows=rows, k=k: arrived(x_all.at[rows, :], a1_sem.at[k]))
        for i in (1, 3, 2):
            device = (ctx, 2 * lax.rem(x + i, 4) + c)
            send(x_all.at[rows, :], x_all.at[rows, :], a2_sem.at[k, i - 1], device, is_remote)
    for i in range(1, 8):
        to = lax.rem(head + i, 8)
        src = w_out.at[:, pl.ds(pl.multiple_of(256 * to, 256), 256)]
        dst = wo_all.at[pl.ds(pl.multiple_of(256 * head, 256), 256), :]
        send(src, dst, wo_sem.at[i - 1], (ctx, to))

    def all_tokens():
        for k in range(2):

            @pl.when(yl != 2 * c + k)
            def _(k=k):
                for i in range(1, 4):
                    rows = pl.ds(pl.multiple_of(RIM + 128 * k + 32 * lax.rem(x + 4 - i, 4), 16), 32)
                    arrived(x_all.at[rows, :], a2_sem.at[k, i - 1])

            pl.when(own_block[k][0])(own_block[k][1].wait)
        arrived(x_all.at[pl.ds(0, RIM), :], rim_sem)

    def multiply(bundle, first):
        rows = x_all[:, pl.ds(pl.multiple_of(256 * bundle, 256), 256)]
        for part in range(2):
            arrived(w_other.at[bundle, cores[part], :], c_sem.at[bundle, part])
        for which, weights in ((c, w_mine), (1 - c, w_other)):
            product = dot(rows, weights[bundle, :256, :], precision=None)
            acc[which] = product if first else acc[which] + product
        small = dot(rows, w_mine[bundle, 256:272, :], ((1,), (1,)), precision=None)
        logit[...] = small if first else logit[...] + small

    for step in range(1, 5):
        below, above = lax.rem(z + 8 - step, 8), lax.rem(z + step, 8)
        for part in range(2):
            for way, bundle in ((0, below), (1, above)):
                if step == 4 and part != way:
                    continue
                arrived(w_mine.at[bundle, chunks[part], :], z_sem.at[way, step - 1, part])
                if step < 3 or (step == 3 and part == way):
                    onward(bundle, step + 1, way, part)
                across(bundle, part)
        if step == 1:
            all_tokens()
            multiply(z, True)
        multiply(below, False)
        if step < 4:
            multiply(above, False)

    arrived(p_other, par_sem)
    settings = jnp.where(hl // 2 == c, p_mine[...], p_other[...])
    second = hl % 2 == 1
    acc[...] = acc[...].astype(BF16).astype(F32)

    def convolved(side, lanes, taps):
        total = acc[side, RIM : RIM + 256, lanes] * taps[3]
        for s in range(3):
            shifted = acc[side, RIM - 3 + s : RIM - 3 + s + 256, lanes]
            total = total + jnp.where(place_of - 3 + s >= start, shifted, 0.0) * taps[s]
        return total * sigmoid(total)

    def pick(low, high):
        return jnp.where(second, settings[high : high + 1], settings[low : low + 1])

    q_act = convolved(0, slice(0, HD), [settings[2 * s : 2 * s + 1] for s in range(4)])
    k_act = convolved(0, slice(HD, 2 * HD), [settings[2 * s + 1 : 2 * s + 2] for s in range(4)])
    v_act = convolved(1, slice(0, HD), [pick(8 + s, 12 + s) for s in range(4)])
    q_act = q_act * (lax.rsqrt(jnp.sum(q_act * q_act, axis=1, keepdims=True) + EPSILON) * HD**-0.5)
    k_act = k_act * lax.rsqrt(jnp.sum(k_act * k_act, axis=1, keepdims=True) + EPSILON)
    logits = logit[RIM:, :]
    beta_logit = jnp.where(second, logits[:, 1:2], logits[:, 0:1])
    decay_logit = jnp.where(second, logits[:, 3:4], logits[:, 2:3])
    beta = jnp.broadcast_to(sigmoid(beta_logit), (256, HD))
    shifted = jnp.broadcast_to(decay_logit, (256, HD)) + pick(17, 19)
    softplus = jnp.maximum(shifted, 0.0) + jnp.log1p(jnp.exp(-jnp.abs(shifted)))
    decay = -pick(16, 18) * softplus

    states, outputs = [], []
    for b in range(2):
        rows = slice(BLOCK * b, BLOCK * b + BLOCK)
        state, solved, ratio, lead = block_state(
            k_act[rows], v_act[rows], beta[rows], decay[rows], start[rows] - BLOCK * b
        )
        states.append(state)
        outputs.append((solved, ratio, lead))
    z_unit[...] = compose(states[0], states[1])
    z_copy = len(pending)
    send(z_unit, z_first, zf_sem, partner, c == 0)

    targets = [(place(group + d, hl), head) for d in range(1, 5)]
    size = [2 * HD, 2 * HD, 2 * HD, HD]

    @pl.when(c == 1)
    def _():
        arrived(z_first, zf_sem)
        z_send[...] = compose(z_first[...], z_unit[...]).astype(BF16)

    for d in range(4):
        part = pl.ds(0, size[d])
        send(z_send.at[part, :], z_in.at[d, part, :], zi_sem.at[d], targets[d], c == 1)

    leads, rests = [], []
    for b in range(2):
        rows = slice(BLOCK * b, BLOCK * b + BLOCK)
        lead_part, rest = block_output(q_act[rows], k_act[rows], *outputs[b])
        if b == 1:
            through = dot(lead_part, states[0], ((1,), (1,)))
            lead_part, rest = through[:, HD:], rest + through[:, :HD]
        leads.append(lead_part)
        rests.append(rest)
    gate = acc[1, RIM:, HD:]
    gate = gate * sigmoid(gate) * gain[...]

    @pl.when(c == 1)
    def _():
        for d in range(4):
            arrived(z_in.at[d, pl.ds(0, size[d]), :], zi_sem.at[d])
        state = z_in[3, :HD].astype(F32)
        for d in (2, 1, 0):
            state = dot(state, z_in[d, HD:].astype(F32)) + z_in[d, :HD].astype(F32)
        s_in[0] = state

    send(s_in.at[0], s_in.at[1], si_sem, partner, c == 1)
    pl.when(c == 0)(lambda: arrived(s_in.at[1], si_sem))

    @pl.when(c == 1)
    def _():
        s_in[1] = dot(s_in[0], z_first[HD:, :]) + z_first[:HD, :]

    before = s_in[1]
    result = dot(jnp.concatenate(leads, axis=0), before, ((1,), (1,))) + jnp.concatenate(rests, axis=0)
    scale = lax.rsqrt(jnp.mean(result * result, axis=1, keepdims=True) + EPSILON)
    n_stage[...] = (result * scale * gate).astype(BF16)

    my_head = 4 * x + hl
    for b in range(2):
        src = n_stage.at[pl.ds(BLOCK * b, BLOCK), :]
        dst = n_all.at[my_head]
        is_self = (yl == 2 * c + b) & (hl % 2 == c)
        device = (4 * group + 2 * c + b, 2 * x + hl % 2)
        send(src, dst, n_sem.at[my_head], device, ~is_self)
        pl.when(is_self)(lambda src=src, dst=dst: pltpu.make_async_copy(src, dst, n_sem.at[my_head]).start())
    for m in range(2):
        which = 4 * x + 2 * m + c
        ref = n_all.at[which]
        arrived(ref, n_sem.at[which])
        for i in (1, 3, 2):
            send(ref, ref, n_sem.at[which], (ctx, 2 * lax.rem(x + i, 4) + c))
        send(ref, ref, n_sem.at[which], partner)
    for i in (1, 3, 2):
        for m in range(2):
            which = 4 * lax.rem(x + i, 4) + 2 * m + c
            ref = n_all.at[which]
            arrived(ref, n_sem.at[which])
            send(ref, ref, n_sem.at[which], partner)
    for i in range(1, 8):
        rows = pl.ds(pl.multiple_of(256 * lax.rem(head + 8 - i, 8), 256), 256)
        arrived(wo_all.at[rows, :], wo_sem.at[i - 1])
    own_out.wait()
    for i in range(8):
        which = 2 * i + 1 - c
        arrived(n_all.at[which], n_sem.at[which])
    total = jnp.zeros((128, 256), F32)
    for i in range(8):
        rows = jnp.concatenate([n_all[2 * i], n_all[2 * i + 1]], axis=1)
        total = total + dot(rows, wo_all[256 * i : 256 * i + 256, :], precision=None)
    out[...] = total.astype(BF16)

    for copy, cond in pending:
        if cond is None:
            copy.wait_send()
        else:
            pl.when(cond)(copy.wait_send)


def local(
    tokens, w_query, w_key, w_value, w_output_gate, w_beta, w_decay, decay_rate, dt_bias, conv_qk, conv_value, norm_gain,
    w_out, doc_lengths,
):
    any_space = pl.BlockSpec(memory_space=pl.ANY)
    vmem = pl.BlockSpec(memory_space=pltpu.VMEM)
    smem = pl.BlockSpec(memory_space=pltpu.SMEM)
    dma = pltpu.SemaphoreType.DMA
    return pl.pallas_call(
        kernel,
        out_shape=jax.ShapeDtypeStruct((128, 256), BF16),
        in_specs=[any_space] + [vmem] * 6 + [smem] * 2 + [vmem] * 3 + [any_space, smem],
        out_specs=vmem,
        scratch_shapes=[
            pltpu.VMEM((RIM + 256, 2048), BF16),
            pltpu.VMEM((8, 272, 256), BF16),
            pltpu.VMEM((8, 256, 256), BF16),
            pltpu.VMEM((2048, 256), BF16),
            pltpu.VMEM((3, 32, 256), BF16),
            pltpu.VMEM((16, HD), BF16),
            pltpu.VMEM((8, 16, HD), BF16),
            pltpu.VMEM((24, HD), F32),
            pltpu.VMEM((24, HD), F32),
            pltpu.VMEM((2, RIM + 256, 256), F32),
            pltpu.VMEM((RIM + 256, 16), F32),
            pltpu.VMEM((2 * HD, HD), F32),
            pltpu.VMEM((2 * HD, HD), F32),
            pltpu.VMEM((2 * HD, HD), BF16),
            pltpu.VMEM((4, 2 * HD, HD), BF16),
            pltpu.VMEM((2, HD, HD), F32),
            pltpu.VMEM((256, HD), BF16),
            pltpu.VMEM((16, 128, HD), BF16),
            dma((110,)),
            dma((2,)),
            dma((2, 3)),
            dma,
            dma((8,)),
            dma((8,)),
            dma((2, 4, 2)),
            dma((8, 2)),
            dma((7,)),
            dma,
            dma,
            dma((4,)),
            dma,
            dma((16,)),
            dma((2,)),
        ],
        compiler_params=pltpu.CompilerParams(
            collective_id=0, has_side_effects=True, vmem_limit_bytes=40 * 2**20
        ),
    )(
        tokens, w_query, w_key, w_value, w_output_gate, w_beta, w_decay, decay_rate, dt_bias, conv_qk, conv_value,
        norm_gain.reshape(1, HD), w_out, doc_lengths,
    )


def solution(mesh):
    return jax.shard_map(
        local,
        mesh=mesh,
        in_specs=(
            P("ctx", None),
            P("ctx", "head"),
            P("ctx", "head"),
            P("ctx", "head"),
            P("ctx", "head"),
            P("ctx", "head"),
            P("ctx", "head"),
            P("head"),
            P("head"),
            P(None, None, "head"),
            P(None, "head"),
            P(),
            P("head", None),
            P(),
        ),
        out_specs=P("ctx", "head"),
        check_vma=False,
    )
```

```python
import jax
import jax.numpy as jnp
from jax import lax
from jax.experimental import pallas as pl
from jax.experimental.pallas import tpu as pltpu
from jax.sharding import PartitionSpec as P

MESH = pl.DeviceIdType.MESH
HIGH = lax.Precision.HIGHEST
EPSILON = 1e-06
HD = 128
BLOCK = 128
RIM = 16
F32 = jnp.float32
BF16 = jnp.bfloat16
FAR = 1 << 20


def dot(a, b, dims=((1,), (0,)), precision=HIGH):
    return lax.dot_general(a, b, (dims, ((), ())), precision=precision, preferred_element_type=F32)


def iota(shape, dim):
    return lax.broadcasted_iota(jnp.int32, shape, dim)


def unit_lower_inverse(lower):
    size = lower.shape[0]
    row, col = iota(lower.shape, 0), iota(lower.shape, 1)
    inverse = jnp.where(row == col, 1.0, 0.0)
    shift = 0
    while (1 << shift) < size:
        joins = ((row >> (shift + 1)) == (col >> (shift + 1))) & ((row >> shift) != (col >> shift))
        part = jnp.where(joins, lower, 0.0)
        if shift == 0:
            inverse = inverse - part
        else:
            inverse = inverse - dot(dot(inverse, part), inverse)
        shift += 1
    return inverse


def block_state(k, v, beta, g, start):
    row, col = iota((BLOCK, BLOCK), 0), iota((BLOCK, BLOCK), 1)
    lower_tri = row >= col
    gam = dot(jnp.where(lower_tri, 1.0, 0.0), g)
    same = lower_tri & (col >= start)
    ratio = jnp.where(same, jnp.exp(jnp.where(same, gam - gam.T, 0.0)), 0.0)
    lead = jnp.where(start < 0, jnp.exp(gam), 0.0)
    inner = dot(k, k, ((1,), (1,)))
    inverse = unit_lower_inverse(jnp.where(row > col, beta * ratio * inner, 0.0))
    solved = dot(inverse, jnp.concatenate([beta * v, beta * lead * k], axis=1))
    tail = jnp.where(row >= start[BLOCK - 1 :], jnp.exp(gam[BLOCK - 1 :] - gam), 0.0)
    joint = dot(solved, tail * k, ((0,), (0,)))
    transition = jnp.where(row == col, lead[BLOCK - 1 :], 0.0) - joint[HD:]
    return jnp.concatenate([joint[:HD], transition], axis=0), solved, ratio, lead


def block_output(q, k, solved, ratio, lead):
    scores = dot(q, k, ((1,), (1,))) * ratio
    mixed = dot(scores, solved)
    return lead * q - mixed[:, HD:], mixed[:, :HD]


def compose(earlier, later):
    joined = dot(earlier, later[HD:])
    return jnp.concatenate([joined[:HD] + later[:HD], joined[HD:]], axis=0)


def sigmoid(x):
    return 1.0 / (1.0 + jnp.exp(-x))


def kernel(
    tokens, w_query, w_key, w_value, w_gate, w_beta, w_decay, rate_in, bias_in, conv_qk_in, conv_value_in, gain_in, w_out,
    docs_in,
    out,
    beta_w, rate, bias, conv_qk, conv_value, gain, docs,
    x_all, w_mine, w_other, wo_all, w_stage, piece, pieces, p_mine, p_other, acc, logit,
    z_unit, z_first, z_send, z_in, s_in, n_stage, n_all,
    send_sem, a1_sem, a2_sem, rim_sem, y_sem, p_sem, z_sem, c_sem, wo_sem, par_sem, zf_sem, zi_sem, si_sem, n_sem, own_sem,
    in_sem,
):
    ctx, head = lax.axis_index("ctx"), lax.axis_index("head")
    z, y = ctx // 8, ctx % 8
    x, c = head // 2, head % 2
    group, yl, yh = ctx // 4, ctx % 4, (ctx % 8) // 4
    hl = jnp.where(yh == 0, y, 7 - y)
    partner = (ctx, 2 * x + 1 - c)

    def place(g, local):
        g = lax.rem(g + 16, 16)
        return 8 * (g // 2) + jnp.where(g % 2 == 0, local, 7 - local)

    pending = []

    def send(src, dst, recv, device, cond=None):
        copy = pltpu.make_async_remote_copy(
            src_ref=src, dst_ref=dst, send_sem=send_sem.at[len(pending)], recv_sem=recv,
            device_id=device, device_id_type=MESH,
        )
        if cond is None:
            copy.start()
        else:
            pl.when(cond)(copy.start)
        pending.append((copy, cond))

    def arrived(dst, sem):
        pltpu.make_async_copy(dst, dst, sem).wait()

    inputs = [
        pltpu.make_async_copy(src, dst, in_sem.at[i])
        for i, (src, dst) in enumerate(
            [
                (w_query, w_stage.at[0, :, :HD]),
                (w_key, w_stage.at[0, :, HD:]),
                (w_value.at[:, :HD], w_stage.at[1, :, :HD]),
                (w_value.at[:, HD:], w_stage.at[2, :, :HD]),
                (w_gate.at[:, :HD], w_stage.at[1, :, HD:]),
                (w_gate.at[:, HD:], w_stage.at[2, :, HD:]),
                (w_beta, beta_w.at[0]),
                (w_decay, beta_w.at[1]),
                (rate_in, rate),
                (bias_in, bias),
                (conv_qk_in, conv_qk),
                (conv_value_in, conv_value),
                (gain_in, gain),
                (docs_in, docs),
            ]
        )
    ]
    for copy in inputs:
        copy.start()

    barrier = pltpu.get_barrier_semaphore()

    def greet(device):
        pl.semaphore_signal(barrier, inc=1, device_id=device, device_id_type=MESH)

    for i in range(1, 8):
        other = 8 * z + lax.rem(y + i, 8)
        greet((other, 2 * x))
        greet((other, 2 * x + 1))
    for i in range(1, 8):
        greet((ctx, lax.rem(head + i, 8)))
    greet((lax.rem(ctx + 8, 64), head))
    greet((lax.rem(ctx + 56, 64), head))
    pl.when((c == 0) & (yh == 0))(lambda: greet((lax.rem(4 * group + 63, 64), 2 * x + 1)))

    @pl.when(c == 1)
    def _():
        for d in range(1, 5):
            greet((place(group - d, hl), head))

    rim_across = (c == 1) & (y == 7)

    for copy in inputs:
        copy.wait()
    for s in range(4):
        for i in range(2):
            p_mine[2 * s + i : 2 * s + i + 1, :] = conv_qk[s, i : i + 1, :]
        for i in range(2):
            p_mine[8 + 4 * i + s : 9 + 4 * i + s, :] = conv_value[s : s + 1, HD * i : HD * i + HD]
    for i in range(2):
        p_mine[16 + 2 * i : 17 + 2 * i, :] = jnp.full((1, HD), rate[i], F32)
        p_mine[17 + 2 * i : 18 + 2 * i, :] = jnp.full((1, HD), bias[i], F32)
    piece[...] = jnp.zeros((16, HD), BF16)
    for q in range(4):

        @pl.when(y % 4 == q)
        def _(q=q):
            piece[0:2, 32 * q : 32 * q + 32] = beta_w[0]
            piece[2:4, 32 * q : 32 * q + 32] = beta_w[1]

    pl.semaphore_wait(barrier, 23 + 4 * c + 4 * rim_across.astype(jnp.int32))

    mine_rows = pl.ds(pl.multiple_of(32 * y, 32), 32)
    selfs = []
    for sub in range(2):
        local = 2 * c + sub
        for half in range(2):
            to = 8 * z + (local if half == 0 else 7 - local)
            me = to == ctx
            for core in range(2):
                device = (to, 2 * x + core)
                src = w_stage.at[0] if core == 0 else w_stage.at[1 + sub]
                is_self = me & (c == core)
                dst = w_mine.at[z, mine_rows, :]
                send(src, dst, y_sem.at[y], device, ~is_self)
                send(piece, pieces.at[y], p_sem.at[y], device, ~is_self)
                selfs.append((src, dst, is_self))
    for src, dst, is_self in selfs:

        @pl.when(is_self)
        def _(src=src, dst=dst):
            pltpu.make_async_copy(src, dst, y_sem.at[y]).start()
            pltpu.make_async_copy(piece, pieces.at[y], p_sem.at[y]).start()

    quarter = pl.ds(pl.multiple_of(32 * x, 32), 32)
    owner = yl // 2 == c
    for i in range(1, 4):
        to = 4 * group + lax.rem(yl + i, 4)
        rows = pl.ds(pl.multiple_of(RIM + 128 * (yl % 2) + 32 * x, 16), 32)
        send(tokens.at[quarter, :], x_all.at[rows, :], a1_sem.at[yl % 2], (to, head), owner)
    after_two = (c == 0) & (yl == 1)
    after_four = (c == 1) & (yl == 3)
    for i in range(4):
        last = tokens.at[pl.ds(128 - RIM, RIM), :]
        to = jnp.where(after_two, 4 * group + i, lax.rem(4 * group + 4 + i, 64))
        send(last, x_all.at[pl.ds(0, RIM), :], rim_sem, (to, 2 * x + 1 - c), after_two | after_four)
    send(p_mine, p_other, par_sem, partner)
    own_block = []
    for k in range(2):
        is_own = yl == 2 * c + k
        block = x_all.at[pl.ds(RIM + 128 * k, 128), :]
        own_block.append((is_own, pltpu.make_async_copy(tokens, block, own_sem.at[0])))
        pl.when(is_own)(own_block[-1][1].start)
    own_out = pltpu.make_async_copy(
        w_out.at[:, pl.ds(pl.multiple_of(256 * head, 256), 256)],
        wo_all.at[pl.ds(pl.multiple_of(256 * head, 256), 256), :],
        own_sem.at[1],
    )
    own_out.start()

    base = 512 * group + 256 * c
    place_of = iota((256, HD), 0)
    start = jnp.full((256, HD), -FAR, jnp.int32)
    offset = -base
    for i in range(32):
        start = jnp.maximum(start, jnp.where(place_of >= offset, offset, -FAR))
        offset = offset + docs[i]

    for i in range(8):
        arrived(w_mine.at[z, pl.ds(32 * i, 32), :], y_sem.at[i])
        arrived(pieces.at[i], p_sem.at[i])
    for i in range(2):
        joined = sum(pieces[4 * i + j].astype(F32) for j in range(4))
        w_mine[z, 256:272, HD * i : HD * i + HD] = joined.astype(BF16)

    ups, downs = lax.rem(ctx + 8, 64), lax.rem(ctx + 56, 64)
    chunks = (pl.ds(0, 144), pl.ds(144, 128))
    cores = (pl.ds(0, 144), pl.ds(144, 112))

    def onward(bundle, step, way, part):
        ref = w_mine.at[bundle, chunks[part], :]
        send(ref, ref, z_sem.at[way, step - 1, part], (ups if way == 0 else downs, head))

    def across(bundle, part):
        send(w_mine.at[bundle, cores[part], :], w_other.at[bundle, cores[part], :], c_sem.at[bundle, part], partner)

    for part in range(2):
        onward(z, 1, 0, part)
        onward(z, 1, 1, part)
    for part in range(2):
        across(z, part)

    for k in range(2):
        is_remote = yl != 2 * c + k
        rows = pl.ds(pl.multiple_of(RIM + 128 * k + 32 * x, 16), 32)
        pl.when(is_remote)(lambda rows=rows, k=k: arrived(x_all.at[rows, :], a1_sem.at[k]))
        for i in (1, 3, 2):
            device = (ctx, 2 * lax.rem(x + i, 4) + c)
            send(x_all.at[rows, :], x_all.at[rows, :], a2_sem.at[k, i - 1], device, is_remote)
    for i in range(1, 8):
        to = lax.rem(head + i, 8)
        src = w_out.at[:, pl.ds(pl.multiple_of(256 * to, 256), 256)]
        dst = wo_all.at[pl.ds(pl.multiple_of(256 * head, 256), 256), :]
        send(src, dst, wo_sem.at[i - 1], (ctx, to))

    def all_tokens():
        for k in range(2):

            @pl.when(yl != 2 * c + k)
            def _(k=k):
                for i in range(1, 4):
                    rows = pl.ds(pl.multiple_of(RIM + 128 * k + 32 * lax.rem(x + 4 - i, 4), 16), 32)
                    arrived(x_all.at[rows, :], a2_sem.at[k, i - 1])

            pl.when(own_block[k][0])(own_block[k][1].wait)
        arrived(x_all.at[pl.ds(0, RIM), :], rim_sem)

    def multiply(bundle, first):
        rows = x_all[:, pl.ds(pl.multiple_of(256 * bundle, 256), 256)]
        for part in range(2):
            arrived(w_other.at[bundle, cores[part], :], c_sem.at[bundle, part])
        for which, weights in ((c, w_mine), (1 - c, w_other)):
            product = dot(rows, weights[bundle, :256, :], precision=None)
            acc[which] = product if first else acc[which] + product
        small = dot(rows, w_mine[bundle, 256:272, :], ((1,), (1,)), precision=None)
        logit[...] = small if first else logit[...] + small

    for step in range(1, 5):
        below, above = lax.rem(z + 8 - step, 8), lax.rem(z + step, 8)
        for part in range(2):
            for way, bundle in ((0, below), (1, above)):
                if step == 4 and part != way:
                    continue
                arrived(w_mine.at[bundle, chunks[part], :], z_sem.at[way, step - 1, part])
                if step < 3 or (step == 3 and part == way):
                    onward(bundle, step + 1, way, part)
                across(bundle, part)
        if step == 1:
            all_tokens()
            multiply(z, True)
        multiply(below, False)
        if step < 4:
            multiply(above, False)

    arrived(p_other, par_sem)
    settings = jnp.where(hl // 2 == c, p_mine[...], p_other[...])
    second = hl % 2 == 1
    acc[...] = acc[...].astype(BF16).astype(F32)

    def convolved(side, lanes, taps):
        total = acc[side, RIM : RIM + 256, lanes] * taps[3]
        for s in range(3):
            shifted = acc[side, RIM - 3 + s : RIM - 3 + s + 256, lanes]
            total = total + jnp.where(place_of - 3 + s >= start, shifted, 0.0) * taps[s]
        return total * sigmoid(total)

    def pick(low, high):
        return jnp.where(second, settings[high : high + 1], settings[low : low + 1])

    q_act = convolved(0, slice(0, HD), [settings[2 * s : 2 * s + 1] for s in range(4)])
    k_act = convolved(0, slice(HD, 2 * HD), [settings[2 * s + 1 : 2 * s + 2] for s in range(4)])
    v_act = convolved(1, slice(0, HD), [pick(8 + s, 12 + s) for s in range(4)])
    q_act = q_act * (lax.rsqrt(jnp.sum(q_act * q_act, axis=1, keepdims=True) + EPSILON) * HD**-0.5)
    k_act = k_act * lax.rsqrt(jnp.sum(k_act * k_act, axis=1, keepdims=True) + EPSILON)
    logits = logit[RIM:, :]
    beta_logit = jnp.where(second, logits[:, 1:2], logits[:, 0:1])
    decay_logit = jnp.where(second, logits[:, 3:4], logits[:, 2:3])
    beta = jnp.broadcast_to(sigmoid(beta_logit), (256, HD))
    shifted = jnp.broadcast_to(decay_logit, (256, HD)) + pick(17, 19)
    softplus = jnp.maximum(shifted, 0.0) + jnp.log1p(jnp.exp(-jnp.abs(shifted)))
    decay = -pick(16, 18) * softplus

    states, outputs = [], []
    for b in range(2):
        rows = slice(BLOCK * b, BLOCK * b + BLOCK)
        state, solved, ratio, lead = block_state(
            k_act[rows], v_act[rows], beta[rows], decay[rows], start[rows] - BLOCK * b
        )
        states.append(state)
        outputs.append((solved, ratio, lead))
    z_unit[...] = compose(states[0], states[1])
    z_copy = len(pending)
    send(z_unit, z_first, zf_sem, partner, c == 0)

    targets = [(place(group + d, hl), head) for d in range(1, 5)]
    size = [2 * HD, 2 * HD, 2 * HD, HD]

    @pl.when(c == 1)
    def _():
        arrived(z_first, zf_sem)
        z_send[...] = compose(z_first[...], z_unit[...]).astype(BF16)

    for d in range(4):
        part = pl.ds(0, size[d])
        send(z_send.at[part, :], z_in.at[d, part, :], zi_sem.at[d], targets[d], c == 1)

    leads, rests = [], []
    for b in range(2):
        rows = slice(BLOCK * b, BLOCK * b + BLOCK)
        lead_part, rest = block_output(q_act[rows], k_act[rows], *outputs[b])
        if b == 1:
            through = dot(lead_part, states[0], ((1,), (1,)))
            lead_part, rest = through[:, HD:], rest + through[:, :HD]
        leads.append(lead_part)
        rests.append(rest)
    gate = acc[1, RIM:, HD:]
    gate = gate * sigmoid(gate) * gain[...]

    @pl.when(c == 1)
    def _():
        for d in range(4):
            arrived(z_in.at[d, pl.ds(0, size[d]), :], zi_sem.at[d])
        state = z_in[3, :HD].astype(F32)
        for d in (2, 1, 0):
            state = dot(state, z_in[d, HD:].astype(F32)) + z_in[d, :HD].astype(F32)
        s_in[0] = state

    send(s_in.at[0], s_in.at[1], si_sem, partner, c == 1)
    pl.when(c == 0)(lambda: arrived(s_in.at[1], si_sem))

    @pl.when(c == 1)
    def _():
        s_in[1] = dot(s_in[0], z_first[HD:, :]) + z_first[:HD, :]

    before = s_in[1]
    result = dot(jnp.concatenate(leads, axis=0), before, ((1,), (1,))) + jnp.concatenate(rests, axis=0)
    scale = lax.rsqrt(jnp.mean(result * result, axis=1, keepdims=True) + EPSILON)
    n_stage[...] = (result * scale * gate).astype(BF16)

    my_head = 4 * x + hl
    for b in range(2):
        src = n_stage.at[pl.ds(BLOCK * b, BLOCK), :]
        dst = n_all.at[my_head]
        is_self = (yl == 2 * c + b) & (hl % 2 == c)
        device = (4 * group + 2 * c + b, 2 * x + hl % 2)
        send(src, dst, n_sem.at[my_head], device, ~is_self)
        pl.when(is_self)(lambda src=src, dst=dst: pltpu.make_async_copy(src, dst, n_sem.at[my_head]).start())
    for m in range(2):
        which = 4 * x + 2 * m + c
        ref = n_all.at[which]
        arrived(ref, n_sem.at[which])
        for i in (1, 3, 2):
            send(ref, ref, n_sem.at[which], (ctx, 2 * lax.rem(x + i, 4) + c))
        send(ref, ref, n_sem.at[which], partner)
    for i in (1, 3, 2):
        for m in range(2):
            which = 4 * lax.rem(x + i, 4) + 2 * m + c
            ref = n_all.at[which]
            arrived(ref, n_sem.at[which])
            send(ref, ref, n_sem.at[which], partner)
    for i in range(1, 8):
        rows = pl.ds(pl.multiple_of(256 * lax.rem(head + 8 - i, 8), 256), 256)
        arrived(wo_all.at[rows, :], wo_sem.at[i - 1])
    own_out.wait()
    for i in range(8):
        which = 2 * i + 1 - c
        arrived(n_all.at[which], n_sem.at[which])
    total = jnp.zeros((128, 256), F32)
    for i in range(8):
        rows = jnp.concatenate([n_all[2 * i], n_all[2 * i + 1]], axis=1)
        total = total + dot(rows, wo_all[256 * i : 256 * i + 256, :], precision=None)
    out[...] = total.astype(BF16)

    for copy, cond in pending:
        if cond is None:
            copy.wait_send()
        else:
            pl.when(cond)(copy.wait_send)


def local(
    tokens, w_query, w_key, w_value, w_output_gate, w_beta, w_decay, decay_rate, dt_bias, conv_qk, conv_value, norm_gain,
    w_out, doc_lengths,
):
    vmem = pl.BlockSpec(memory_space=pltpu.VMEM)
    dma = pltpu.SemaphoreType.DMA
    return pl.pallas_call(
        kernel,
        out_shape=jax.ShapeDtypeStruct((128, 256), BF16),
        in_specs=[pl.BlockSpec(memory_space=pltpu.HBM)] * 14,
        out_specs=vmem,
        scratch_shapes=[
            pltpu.VMEM((2, 2, 32), BF16),
            pltpu.SMEM((2,), F32),
            pltpu.SMEM((2,), F32),
            pltpu.VMEM((4, 2, HD), F32),
            pltpu.VMEM((4, 256), F32),
            pltpu.VMEM((1, HD), F32),
            pltpu.SMEM((32,), jnp.int32),
            pltpu.VMEM((RIM + 256, 2048), BF16),
            pltpu.VMEM((8, 272, 256), BF16),
            pltpu.VMEM((8, 256, 256), BF16),
            pltpu.VMEM((2048, 256), BF16),
            pltpu.VMEM((3, 32, 256), BF16),
            pltpu.VMEM((16, HD), BF16),
            pltpu.VMEM((8, 16, HD), BF16),
            pltpu.VMEM((24, HD), F32),
            pltpu.VMEM((24, HD), F32),
            pltpu.VMEM((2, RIM + 256, 256), F32),
            pltpu.VMEM((RIM + 256, 16), F32),
            pltpu.VMEM((2 * HD, HD), F32),
            pltpu.VMEM((2 * HD, HD), F32),
            pltpu.VMEM((2 * HD, HD), BF16),
            pltpu.VMEM((4, 2 * HD, HD), BF16),
            pltpu.VMEM((2, HD, HD), F32),
            pltpu.VMEM((256, HD), BF16),
            pltpu.VMEM((16, 128, HD), BF16),
            dma((110,)),
            dma((2,)),
            dma((2, 3)),
            dma,
            dma((8,)),
            dma((8,)),
            dma((2, 4, 2)),
            dma((8, 2)),
            dma((7,)),
            dma,
            dma,
            dma((4,)),
            dma,
            dma((16,)),
            dma((2,)),
            dma((14,)),
        ],
        compiler_params=pltpu.CompilerParams(
            collective_id=0, has_side_effects=True, vmem_limit_bytes=60 * 2**20
        ),
    )(
        tokens, w_query, w_key, w_value, w_output_gate, w_beta.T, w_decay.T, decay_rate, dt_bias, conv_qk, conv_value,
        norm_gain.reshape(1, HD), w_out, doc_lengths,
    )


def solution(mesh):
    return jax.shard_map(
        local,
        mesh=mesh,
        in_specs=(
            P("ctx", None),
            P("ctx", "head"),
            P("ctx", "head"),
            P("ctx", "head"),
            P("ctx", "head"),
            P("ctx", "head"),
            P("ctx", "head"),
            P("head"),
            P("head"),
            P(None, None, "head"),
            P(None, "head"),
            P(),
            P("head", None),
            P(),
        ),
        out_specs=P("ctx", "head"),
        check_vma=False,
    )
```

```python
import jax
import jax.numpy as jnp
from jax import lax
from jax.experimental import pallas as pl
from jax.experimental.pallas import tpu as pltpu
from jax.sharding import PartitionSpec as P

MESH = pl.DeviceIdType.MESH
EPSILON = 1e-06
HD = 128
BLOCK = 128
RIM = 16
F32 = jnp.float32
BF16 = jnp.bfloat16
FAR = 1 << 20


def dot(a, b, dims=((1,), (0,))):
    return lax.dot_general(a, b, (dims, ((), ())), preferred_element_type=F32)


def halves(a):
    high = a.astype(BF16)
    return high, (a - high.astype(F32)).astype(BF16)


def dot3(a, b):
    width = b.shape[1]
    (a_high, a_low), (b_high, b_low) = halves(a), halves(b)
    left = jnp.concatenate([a_high, a_low], axis=1)
    right = jnp.concatenate(
        [jnp.concatenate([b_high, b_low], axis=1), jnp.concatenate([b_high, jnp.zeros_like(b_low)], axis=1)], axis=0
    )
    both = dot(left, right)
    return both[:, :width] + both[:, width:]


def dot2(a, b):
    width = b.shape[1]
    both = dot(a, jnp.concatenate(halves(b), axis=1))
    return both[:, :width] + both[:, width:]


def iota(shape, dim):
    return lax.broadcasted_iota(jnp.int32, shape, dim)


def each(function, *lists):
    return [function(*items) for items in zip(*lists)]


def unit_lower_inverses(lowers):
    size = lowers[0].shape[0]
    row, col = iota((size, size), 0), iota((size, size), 1)
    inverses = each(lambda lower: jnp.where(row == col, 1.0, 0.0), lowers)
    shift = 0
    while (1 << shift) < size:
        joins = ((row >> (shift + 1)) == (col >> (shift + 1))) & ((row >> shift) != (col >> shift))
        parts = each(lambda lower: jnp.where(joins, lower, 0.0), lowers)
        if shift > 0:
            parts = each(dot3, each(dot3, inverses, parts), inverses)
        inverses = each(lambda inverse, part: inverse - part, inverses, parts)
        shift += 1
    return inverses


def block_states(k, v, beta, g, start):
    row, col = iota((BLOCK, BLOCK), 0), iota((BLOCK, BLOCK), 1)
    lower_tri = row >= col
    ones = jnp.where(lower_tri, 1.0, 0.0).astype(BF16)
    gam = each(lambda g: dot2(ones, g), g)
    inner = each(lambda k: dot3(k, k.T), k)
    ratio, lead, lower = [], [], []
    for b in range(len(k)):
        same = lower_tri & (col >= start[b])
        ratio.append(jnp.where(same, jnp.exp(jnp.where(same, gam[b] - gam[b].T, 0.0)), 0.0))
        lead.append(jnp.where(start[b] < 0, jnp.exp(gam[b]), 0.0))
        lower.append(jnp.where(row > col, beta[b] * ratio[b] * inner[b], 0.0))
    rights, lasts = [], []
    for b in range(len(k)):
        rights.append(jnp.concatenate([beta[b] * v[b], beta[b] * lead[b] * k[b]], axis=1))
        tail = jnp.where(row >= start[b][BLOCK - 1 :], jnp.exp(gam[b][BLOCK - 1 :] - gam[b]), 0.0)
        lasts.append((tail * k[b]).T)
    inverses = unit_lower_inverses(lower)
    solved = each(dot3, inverses, rights)
    joint = each(dot3, lasts, solved)
    states = []
    for b in range(len(k)):
        transition = jnp.where(row == col, lead[b][BLOCK - 1 :], 0.0) - joint[b][:, HD:]
        states.append(jnp.concatenate([joint[b][:, :HD], transition], axis=1))
    return states, solved, ratio, lead


def compose(earlier, later):
    joined = dot3(later[:, HD:], earlier)
    return jnp.concatenate([joined[:, :HD] + later[:, :HD], joined[:, HD:]], axis=1)


def sigmoid(x):
    return 1.0 / (1.0 + jnp.exp(-x))


def kernel(
    tokens, w_query, w_key, w_value, w_gate, w_beta, w_decay, rate_in, bias_in, conv_qk_in, conv_value_in, gain_in, w_out,
    docs_in,
    out,
    beta_w, rate, bias, conv_qk, conv_value, gain, docs,
    x_all, w_mine, w_other, wo_all, w_stage, piece, pieces, p_mine, p_other, acc, logit,
    z_unit, z_first, z_send, z_in, s_in, n_stage, n_all,
    send_sem, a1_sem, a2_sem, rim_sem, y_sem, p_sem, z_sem, c_sem, wo_sem, par_sem, zf_sem, zi_sem, si_sem, n_sem, own_sem,
    in_sem,
):
    ctx, head = lax.axis_index("ctx"), lax.axis_index("head")
    z, y = ctx // 8, ctx % 8
    x, c = head // 2, head % 2
    group, yl, yh = ctx // 4, ctx % 4, (ctx % 8) // 4
    hl = jnp.where(yh == 0, y, 7 - y)
    partner = (ctx, 2 * x + 1 - c)

    def place(g, local):
        g = lax.rem(g + 16, 16)
        return 8 * (g // 2) + jnp.where(g % 2 == 0, local, 7 - local)

    pending = []

    def send(src, dst, recv, device, cond=None):
        copy = pltpu.make_async_remote_copy(
            src_ref=src, dst_ref=dst, send_sem=send_sem.at[len(pending)], recv_sem=recv,
            device_id=device, device_id_type=MESH,
        )
        if cond is None:
            copy.start()
        else:
            pl.when(cond)(copy.start)
        pending.append((copy, cond))

    def sent(copy, cond):
        if cond is None:
            copy.wait_send()
        else:
            pl.when(cond)(copy.wait_send)

    def arrived(dst, sem):
        pltpu.make_async_copy(dst, dst, sem).wait()

    barrier = pltpu.get_barrier_semaphore()

    def greet(device):
        pl.semaphore_signal(barrier, inc=1, device_id=device, device_id_type=MESH)

    for i in range(1, 8):
        other = 8 * z + lax.rem(y + i, 8)
        greet((other, 2 * x))
        greet((other, 2 * x + 1))
    for i in range(1, 8):
        greet((ctx, lax.rem(head + i, 8)))
    greet((lax.rem(ctx + 8, 64), head))
    greet((lax.rem(ctx + 56, 64), head))
    pl.when((c == 0) & (yh == 0))(lambda: greet((lax.rem(4 * group + 63, 64), 2 * x + 1)))

    @pl.when(c == 1)
    def _():
        for d in range(1, 5):
            greet((place(group - d, hl), head))

    rim_across = (c == 1) & (y == 7)

    inputs = [
        pltpu.make_async_copy(src, dst, in_sem.at[i])
        for i, (src, dst) in enumerate(
            [
                (w_query, w_stage.at[0, :, :HD]),
                (w_key, w_stage.at[0, :, HD:]),
                (w_value.at[:, :HD], w_stage.at[1, :, :HD]),
                (w_value.at[:, HD:], w_stage.at[2, :, :HD]),
                (w_gate.at[:, :HD], w_stage.at[1, :, HD:]),
                (w_gate.at[:, HD:], w_stage.at[2, :, HD:]),
                (w_beta, beta_w.at[0]),
                (w_decay, beta_w.at[1]),
                (rate_in, rate),
                (bias_in, bias),
                (conv_qk_in, conv_qk),
                (conv_value_in, conv_value),
                (gain_in, gain),
                (docs_in, docs),
            ]
        )
    ]
    for copy in inputs:
        copy.start()

    for copy in inputs:
        copy.wait()
    for s in range(4):
        for i in range(2):
            p_mine[2 * s + i : 2 * s + i + 1, :] = conv_qk[s, i : i + 1, :]
        for i in range(2):
            p_mine[8 + 4 * i + s : 9 + 4 * i + s, :] = conv_value[s : s + 1, HD * i : HD * i + HD]
    for i in range(2):
        p_mine[16 + 2 * i : 17 + 2 * i, :] = jnp.full((1, HD), rate[i], F32)
        p_mine[17 + 2 * i : 18 + 2 * i, :] = jnp.full((1, HD), bias[i], F32)
    piece[...] = jnp.zeros((16, HD), BF16)
    for q in range(4):

        @pl.when(y % 4 == q)
        def _(q=q):
            piece[0:2, 32 * q : 32 * q + 32] = beta_w[0]
            piece[2:4, 32 * q : 32 * q + 32] = beta_w[1]

    pl.semaphore_wait(barrier, 23 + 4 * c + 4 * rim_across.astype(jnp.int32))

    mine_rows = pl.ds(pl.multiple_of(32 * y, 32), 32)
    selfs = []
    for sub in range(2):
        local = 2 * c + sub
        for half in range(2):
            to = 8 * z + (local if half == 0 else 7 - local)
            me = to == ctx
            for core in range(2):
                device = (to, 2 * x + core)
                src = w_stage.at[0] if core == 0 else w_stage.at[1 + sub]
                is_self = me & (c == core)
                dst = w_mine.at[z, mine_rows, :]
                send(src, dst, y_sem.at[y], device, ~is_self)
                send(piece, pieces.at[y], p_sem.at[y], device, ~is_self)
                selfs.append((src, dst, is_self))
    for src, dst, is_self in selfs:

        @pl.when(is_self)
        def _(src=src, dst=dst):
            pltpu.make_async_copy(src, dst, y_sem.at[y]).start()
            pltpu.make_async_copy(piece, pieces.at[y], p_sem.at[y]).start()

    def tokens_out():
        quarter = pl.ds(pl.multiple_of(32 * x, 32), 32)
        owner = yl // 2 == c
        for i in range(1, 4):
            to = 4 * group + lax.rem(yl + i, 4)
            rows = pl.ds(pl.multiple_of(RIM + 128 * (yl % 2) + 32 * x, 16), 32)
            send(tokens.at[quarter, :], x_all.at[rows, :], a1_sem.at[yl % 2], (to, head), owner)
        after_two = (c == 0) & (yl == 1)
        after_four = (c == 1) & (yl == 3)
        for i in range(4):
            last = tokens.at[pl.ds(128 - RIM, RIM), :]
            to = jnp.where(after_two, 4 * group + i, lax.rem(4 * group + 4 + i, 64))
            send(last, x_all.at[pl.ds(0, RIM), :], rim_sem, (to, 2 * x + 1 - c), after_two | after_four)

    send(p_mine, p_other, par_sem, partner)
    own_block = []
    for k in range(2):
        is_own = yl == 2 * c + k
        block = x_all.at[pl.ds(RIM + 128 * k, 128), :]
        own_block.append((is_own, pltpu.make_async_copy(tokens, block, own_sem.at[0])))
        pl.when(is_own)(own_block[-1][1].start)
    own_out = pltpu.make_async_copy(
        w_out.at[:, pl.ds(pl.multiple_of(256 * head, 256), 256)],
        wo_all.at[pl.ds(pl.multiple_of(256 * head, 256), 256), :],
        own_sem.at[1],
    )
    own_out.start()

    base = 512 * group + 256 * c
    place_of = iota((256, HD), 0)
    start = jnp.full((256, HD), -FAR, jnp.int32)
    offset = -base
    for i in range(32):
        start = jnp.maximum(start, jnp.where(place_of >= offset, offset, -FAR))
        offset = offset + docs[i]

    for i in range(8):
        arrived(w_mine.at[z, pl.ds(32 * i, 32), :], y_sem.at[i])
        arrived(pieces.at[i], p_sem.at[i])
    for i in range(2):
        joined = sum(pieces[4 * i + j].astype(F32) for j in range(4))
        w_mine[z, 256:272, HD * i : HD * i + HD] = joined.astype(BF16)

    ups, downs = lax.rem(ctx + 8, 64), lax.rem(ctx + 56, 64)
    chunks = [pl.ds(at, size) for at, size in ((0, 80), (80, 64), (144, 64), (208, 64))]
    cores = (pl.ds(0, 144), pl.ds(144, 112))

    def onward(bundle, step, way, part):
        ref = w_mine.at[bundle, chunks[part], :]
        send(ref, ref, z_sem.at[way, step - 1, part], (ups if way == 0 else downs, head))

    def across(bundle, part):
        send(w_mine.at[bundle, cores[part], :], w_other.at[bundle, cores[part], :], c_sem.at[bundle, part], partner)

    for part in range(4):
        onward(z, 1, 0, part)
        onward(z, 1, 1, part)
    for part in range(2):
        across(z, part)

    tokens_out()
    def tokens_on():
        for k in range(2):
            is_remote = yl != 2 * c + k
            rows = pl.ds(pl.multiple_of(RIM + 128 * k + 32 * x, 16), 32)
            pl.when(is_remote)(lambda rows=rows, k=k: arrived(x_all.at[rows, :], a1_sem.at[k]))
            for i in (1, 3, 2):
                device = (ctx, 2 * lax.rem(x + i, 4) + c)
                send(x_all.at[rows, :], x_all.at[rows, :], a2_sem.at[k, i - 1], device, is_remote)
        for i in range(1, 8):
            to = lax.rem(head + i, 8)
            src = w_out.at[:, pl.ds(pl.multiple_of(256 * to, 256), 256)]
            dst = wo_all.at[pl.ds(pl.multiple_of(256 * head, 256), 256), :]
            send(src, dst, wo_sem.at[i - 1], (ctx, to))

    def all_tokens():
        for k in range(2):

            @pl.when(yl != 2 * c + k)
            def _(k=k):
                for i in range(1, 4):
                    rows = pl.ds(pl.multiple_of(RIM + 128 * k + 32 * lax.rem(x + 4 - i, 4), 16), 32)
                    arrived(x_all.at[rows, :], a2_sem.at[k, i - 1])

            pl.when(own_block[k][0])(own_block[k][1].wait)
        arrived(x_all.at[pl.ds(0, RIM), :], rim_sem)

    def multiply(bundle, first):
        rows = x_all[:, pl.ds(pl.multiple_of(256 * bundle, 256), 256)]
        for part in range(2):
            arrived(w_other.at[bundle, cores[part], :], c_sem.at[bundle, part])
        for which, weights in ((c, w_mine), (1 - c, w_other)):
            product = dot(rows, weights[bundle, :256, :])
            acc[which] = product if first else acc[which] + product
        small = dot(rows, w_mine[bundle, 256:272, :], ((1,), (1,)))
        logit[...] = small if first else logit[...] + small

    for step in range(1, 5):
        below, above = lax.rem(z + 8 - step, 8), lax.rem(z + step, 8)
        for part in range(4):
            for way, bundle in ((0, below), (1, above)):
                if step == 4 and part // 2 != way:
                    continue
                arrived(w_mine.at[bundle, chunks[part], :], z_sem.at[way, step - 1, part])
                if step < 3 or (step == 3 and part // 2 == way):
                    onward(bundle, step + 1, way, part)
                if part % 2 == 1:
                    across(bundle, part // 2)
        if step == 1:
            tokens_on()
        if step == 3:
            all_tokens()
            multiply(z, True)
            for near in range(1, 3):
                multiply(lax.rem(z + 8 - near, 8), False)
                multiply(lax.rem(z + near, 8), False)
        if step >= 3:
            multiply(below, False)
            if step < 4:
                multiply(above, False)

    arrived(p_other, par_sem)
    settings = jnp.where(hl // 2 == c, p_mine[...], p_other[...])
    second = hl % 2 == 1
    acc[...] = acc[...].astype(BF16).astype(F32)

    def convolved(side, lanes, taps):
        total = acc[side, RIM : RIM + 256, lanes] * taps[3]
        for s in range(3):
            shifted = acc[side, RIM - 3 + s : RIM - 3 + s + 256, lanes]
            total = total + jnp.where(place_of - 3 + s >= start, shifted, 0.0) * taps[s]
        return total * sigmoid(total)

    def pick(low, high):
        return jnp.where(second, settings[high : high + 1], settings[low : low + 1])

    q_act = convolved(0, slice(0, HD), [settings[2 * s : 2 * s + 1] for s in range(4)])
    k_act = convolved(0, slice(HD, 2 * HD), [settings[2 * s + 1 : 2 * s + 2] for s in range(4)])
    v_act = convolved(1, slice(0, HD), [pick(8 + s, 12 + s) for s in range(4)])
    q_act = q_act * (lax.rsqrt(jnp.sum(q_act * q_act, axis=1, keepdims=True) + EPSILON) * HD**-0.5)
    k_act = k_act * lax.rsqrt(jnp.sum(k_act * k_act, axis=1, keepdims=True) + EPSILON)
    logits = logit[RIM:, :]
    beta_logit = jnp.where(second, logits[:, 1:2], logits[:, 0:1])
    decay_logit = jnp.where(second, logits[:, 3:4], logits[:, 2:3])
    beta = jnp.broadcast_to(sigmoid(beta_logit), (256, HD))
    shifted = jnp.broadcast_to(decay_logit, (256, HD)) + pick(17, 19)
    softplus = jnp.maximum(shifted, 0.0) + jnp.log1p(jnp.exp(-jnp.abs(shifted)))
    decay = -pick(16, 18) * softplus

    def blocks(array):
        return [array[:BLOCK], array[BLOCK:]]

    q_two, k_two, start_two = blocks(q_act), blocks(k_act), blocks(start)
    states, solved, ratio, lead = block_states(
        k_two, blocks(v_act), blocks(beta), blocks(decay), [start_two[0], start_two[1] - BLOCK]
    )
    z_unit[...] = compose(states[0], states[1])
    send(z_unit, z_first, zf_sem, partner, c == 0)

    targets = [(place(group + d, hl), head) for d in range(1, 5)]
    size = [2 * HD, 2 * HD, 2 * HD, HD]

    @pl.when(c == 1)
    def _():
        arrived(z_first, zf_sem)
        z_send[...] = compose(z_first[...], z_unit[...]).astype(BF16)

    for d in range(4):
        part = pl.ds(0, size[d])
        send(z_send.at[:, part], z_in.at[d, :, part], zi_sem.at[d], targets[d], c == 1)

    scores = each(lambda q, k, ratio: dot3(q, k.T) * ratio, q_two, k_two, ratio)
    mixed = each(dot3, scores, solved)
    leads = each(lambda q, lead, mixed: lead * q - mixed[:, HD:], q_two, lead, mixed)
    rests = each(lambda mixed: mixed[:, :HD], mixed)
    through = dot3(leads[1], states[0])
    leads[1], rests[1] = through[:, HD:], rests[1] + through[:, :HD]
    lead_all, rest_all = jnp.concatenate(leads, axis=0), jnp.concatenate(rests, axis=0)
    gate = acc[1, RIM:, HD:]
    gate = gate * sigmoid(gate) * gain[...]
    done = len(pending) - 5
    for copy, cond in pending[:done]:
        sent(copy, cond)

    @pl.when(c == 1)
    def _():
        for d in range(4):
            arrived(z_in.at[d, :, pl.ds(0, size[d])], zi_sem.at[d])
        state = z_in[3, :, :HD].astype(F32)
        for d in (2, 1, 0):
            state = dot2(z_in[d, :, HD:], state) + z_in[d, :, :HD].astype(F32)
        s_in[0] = state

    send(s_in.at[0], s_in.at[1], si_sem, partner, c == 1)
    pl.when(c == 0)(lambda: arrived(s_in.at[1], si_sem))

    @pl.when(c == 1)
    def _():
        s_in[1] = dot3(z_first[:, HD:], s_in[0]) + z_first[:, :HD]

    before = s_in[1]
    result = dot3(lead_all, before) + rest_all
    scale = lax.rsqrt(jnp.mean(result * result, axis=1, keepdims=True) + EPSILON)
    n_stage[...] = (result * scale * gate).astype(BF16)

    my_head = 4 * x + hl
    for b in range(2):
        src = n_stage.at[pl.ds(BLOCK * b, BLOCK), :]
        dst = n_all.at[my_head]
        is_self = (yl == 2 * c + b) & (hl % 2 == c)
        device = (4 * group + 2 * c + b, 2 * x + hl % 2)
        send(src, dst, n_sem.at[my_head], device, ~is_self)
        pl.when(is_self)(lambda src=src, dst=dst: pltpu.make_async_copy(src, dst, n_sem.at[my_head]).start())
    for m in range(2):
        which = 4 * x + 2 * m + c
        ref = n_all.at[which]
        arrived(ref, n_sem.at[which])
        for i in (1, 3, 2):
            send(ref, ref, n_sem.at[which], (ctx, 2 * lax.rem(x + i, 4) + c))
        send(ref, ref, n_sem.at[which], partner)
    for i in (1, 3, 2):
        for m in range(2):
            which = 4 * lax.rem(x + i, 4) + 2 * m + c
            ref = n_all.at[which]
            arrived(ref, n_sem.at[which])
            send(ref, ref, n_sem.at[which], partner)
    for i in range(1, 8):
        rows = pl.ds(pl.multiple_of(256 * lax.rem(head + 8 - i, 8), 256), 256)
        arrived(wo_all.at[rows, :], wo_sem.at[i - 1])
    own_out.wait()
    for i in range(8):
        which = 2 * i + 1 - c
        arrived(n_all.at[which], n_sem.at[which])
    total = jnp.zeros((128, 256), F32)
    for i in range(8):
        rows = jnp.concatenate([n_all[2 * i], n_all[2 * i + 1]], axis=1)
        total = total + dot(rows, wo_all[256 * i : 256 * i + 256, :])
    out[...] = total.astype(BF16)

    for copy, cond in pending[done:]:
        sent(copy, cond)


def local(
    tokens, w_query, w_key, w_value, w_output_gate, w_beta, w_decay, decay_rate, dt_bias, conv_qk, conv_value, norm_gain,
    w_out, doc_lengths,
):
    vmem = pl.BlockSpec(memory_space=pltpu.VMEM)
    dma = pltpu.SemaphoreType.DMA
    return pl.pallas_call(
        kernel,
        out_shape=jax.ShapeDtypeStruct((128, 256), BF16),
        in_specs=[pl.BlockSpec(memory_space=pltpu.HBM)] * 14,
        out_specs=vmem,
        scratch_shapes=[
            pltpu.VMEM((2, 2, 32), BF16),
            pltpu.SMEM((2,), F32),
            pltpu.SMEM((2,), F32),
            pltpu.VMEM((4, 2, HD), F32),
            pltpu.VMEM((4, 256), F32),
            pltpu.VMEM((1, HD), F32),
            pltpu.SMEM((32,), jnp.int32),
            pltpu.VMEM((RIM + 256, 2048), BF16),
            pltpu.VMEM((8, 272, 256), BF16),
            pltpu.VMEM((8, 256, 256), BF16),
            pltpu.VMEM((2048, 256), BF16),
            pltpu.VMEM((3, 32, 256), BF16),
            pltpu.VMEM((16, HD), BF16),
            pltpu.VMEM((8, 16, HD), BF16),
            pltpu.VMEM((24, HD), F32),
            pltpu.VMEM((24, HD), F32),
            pltpu.VMEM((2, RIM + 256, 256), F32),
            pltpu.VMEM((RIM + 256, 16), F32),
            pltpu.VMEM((HD, 2 * HD), F32),
            pltpu.VMEM((HD, 2 * HD), F32),
            pltpu.VMEM((HD, 2 * HD), BF16),
            pltpu.VMEM((4, HD, 2 * HD), BF16),
            pltpu.VMEM((2, HD, HD), F32),
            pltpu.VMEM((256, HD), BF16),
            pltpu.VMEM((16, 128, HD), BF16),
            dma((128,)),
            dma((2,)),
            dma((2, 3)),
            dma,
            dma((8,)),
            dma((8,)),
            dma((2, 4, 4)),
            dma((8, 2)),
            dma((7,)),
            dma,
            dma,
            dma((4,)),
            dma,
            dma((16,)),
            dma((2,)),
            dma((14,)),
        ],
        compiler_params=pltpu.CompilerParams(
            collective_id=0, has_side_effects=True, vmem_limit_bytes=60 * 2**20
        ),
    )(
        tokens, w_query, w_key, w_value, w_output_gate, w_beta.T, w_decay.T, decay_rate, dt_bias, conv_qk, conv_value,
        norm_gain.reshape(1, HD), w_out, doc_lengths,
    )


def solution(mesh):
    return jax.shard_map(
        local,
        mesh=mesh,
        in_specs=(
            P("ctx", None),
            P("ctx", "head"),
            P("ctx", "head"),
            P("ctx", "head"),
            P("ctx", "head"),
            P("ctx", "head"),
            P("ctx", "head"),
            P("head"),
            P("head"),
            P(None, None, "head"),
            P(None, "head"),
            P(),
            P("head", None),
            P(),
        ),
        out_specs=P("ctx", "head"),
        check_vma=False,
    )
```

```python
import jax
import jax.numpy as jnp
from jax import lax
from jax.experimental import pallas as pl
from jax.experimental.pallas import tpu as pltpu
from jax.sharding import PartitionSpec as P

MESH = pl.DeviceIdType.MESH
EPSILON = 1e-06
HD = 128
BLOCK = 128
RIM = 16
F32 = jnp.float32
BF16 = jnp.bfloat16
FAR = 1 << 20


def dot(a, b, dims=((1,), (0,))):
    return lax.dot_general(a, b, (dims, ((), ())), preferred_element_type=F32)


def halves(a):
    high = a.astype(BF16)
    return high, (a - high.astype(F32)).astype(BF16)


def dot3(a, b):
    width = b.shape[1]
    (a_high, a_low), (b_high, b_low) = halves(a), halves(b)
    left = jnp.concatenate([a_high, a_low], axis=1)
    right = jnp.concatenate(
        [jnp.concatenate([b_high, b_low], axis=1), jnp.concatenate([b_high, jnp.zeros_like(b_low)], axis=1)], axis=0
    )
    both = dot(left, right)
    return both[:, :width] + both[:, width:]


def dot2(a, b):
    width = b.shape[1]
    both = dot(a, jnp.concatenate(halves(b), axis=1))
    return both[:, :width] + both[:, width:]


def iota(shape, dim):
    return lax.broadcasted_iota(jnp.int32, shape, dim)


def each(function, *lists):
    return [function(*items) for items in zip(*lists)]


def unit_lower_inverses(lowers):
    size = lowers[0].shape[0]
    row, col = iota((size, size), 0), iota((size, size), 1)
    inverses = each(lambda lower: jnp.where(row == col, 1.0, 0.0), lowers)
    shift = 0
    while (1 << shift) < size:
        joins = ((row >> (shift + 1)) == (col >> (shift + 1))) & ((row >> shift) != (col >> shift))
        parts = each(lambda lower: jnp.where(joins, lower, 0.0), lowers)
        if shift > 0:
            parts = each(dot3, each(dot3, inverses, parts), inverses)
        inverses = each(lambda inverse, part: inverse - part, inverses, parts)
        shift += 1
    return inverses


def block_states(k, v, beta, g, start):
    row, col = iota((BLOCK, BLOCK), 0), iota((BLOCK, BLOCK), 1)
    lower_tri = row >= col
    ones = jnp.where(lower_tri, 1.0, 0.0).astype(BF16)
    gam = each(lambda g: dot2(ones, g), g)
    inner = each(lambda k: dot3(k, k.T), k)
    ratio, lead, lower = [], [], []
    for b in range(len(k)):
        same = lower_tri & (col >= start[b])
        ratio.append(jnp.where(same, jnp.exp(jnp.where(same, gam[b] - gam[b].T, 0.0)), 0.0))
        lead.append(jnp.where(start[b] < 0, jnp.exp(gam[b]), 0.0))
        lower.append(jnp.where(row > col, beta[b] * ratio[b] * inner[b], 0.0))
    rights, lasts = [], []
    for b in range(len(k)):
        rights.append(jnp.concatenate([beta[b] * v[b], beta[b] * lead[b] * k[b]], axis=1))
        tail = jnp.where(row >= start[b][BLOCK - 1 :], jnp.exp(gam[b][BLOCK - 1 :] - gam[b]), 0.0)
        lasts.append((tail * k[b]).T)
    inverses = unit_lower_inverses(lower)
    solved = each(dot3, inverses, rights)
    joint = each(dot3, lasts, solved)
    states = []
    for b in range(len(k)):
        transition = jnp.where(row == col, lead[b][BLOCK - 1 :], 0.0) - joint[b][:, HD:]
        states.append(jnp.concatenate([joint[b][:, :HD], transition], axis=1))
    return states, solved, ratio, lead


def compose(earlier, later):
    joined = dot3(later[:, HD:], earlier)
    return jnp.concatenate([joined[:, :HD] + later[:, :HD], joined[:, HD:]], axis=1)


def sigmoid(x):
    return 1.0 / (1.0 + jnp.exp(-x))


def kernel(
    tokens, w_query, w_key, w_value, w_gate, w_beta, w_decay, rate_in, bias_in, conv_qk_in, conv_value_in, gain_in, w_out,
    docs_in,
    out,
    beta_w, rate, bias, conv_qk, conv_value, gain, docs,
    x_all, w_mine, w_other, wo_all, w_stage, piece, pieces, p_mine, p_other, acc, logit,
    z_unit, z_first, z_send, z_in, s_in, n_stage, n_all,
    send_sem, a1_sem, a2_sem, rim_sem, y_sem, p_sem, z_sem, c_sem, wo_sem, par_sem, zf_sem, zi_sem, si_sem, n_sem, own_sem,
    in_sem,
):
    ctx, head = lax.axis_index("ctx"), lax.axis_index("head")
    z, y = ctx // 8, ctx % 8
    x, c = head // 2, head % 2
    group, yl, yh = ctx // 4, ctx % 4, (ctx % 8) // 4
    hl = jnp.where(yh == 0, y, 7 - y)
    partner = (ctx, 2 * x + 1 - c)

    def place(g, local):
        g = lax.rem(g + 16, 16)
        return 8 * (g // 2) + jnp.where(g % 2 == 0, local, 7 - local)

    pending = []

    def send(src, dst, recv, device, cond=None):
        copy = pltpu.make_async_remote_copy(
            src_ref=src, dst_ref=dst, send_sem=send_sem.at[len(pending)], recv_sem=recv,
            device_id=device, device_id_type=MESH,
        )
        if cond is None:
            copy.start()
        else:
            pl.when(cond)(copy.start)
        pending.append((copy, cond))

    def sent(copy, cond):
        if cond is None:
            copy.wait_send()
        else:
            pl.when(cond)(copy.wait_send)

    def arrived(dst, sem):
        pltpu.make_async_copy(dst, dst, sem).wait()

    inputs = [
        pltpu.make_async_copy(src, dst, in_sem.at[i])
        for i, (src, dst) in enumerate(
            [
                (w_query, w_stage.at[0, :, :HD]),
                (w_key, w_stage.at[0, :, HD:]),
                (w_value.at[:, :HD], w_stage.at[1, :, :HD]),
                (w_value.at[:, HD:], w_stage.at[2, :, :HD]),
                (w_gate.at[:, :HD], w_stage.at[1, :, HD:]),
                (w_gate.at[:, HD:], w_stage.at[2, :, HD:]),
                (w_beta, beta_w.at[0]),
                (w_decay, beta_w.at[1]),
                (rate_in, rate),
                (bias_in, bias),
                (conv_qk_in, conv_qk),
                (conv_value_in, conv_value),
                (gain_in, gain),
                (docs_in, docs),
            ]
        )
    ]
    for copy in inputs[:8]:
        copy.start()

    barrier = pltpu.get_barrier_semaphore()

    def greet(device):
        pl.semaphore_signal(barrier, inc=1, device_id=device, device_id_type=MESH)

    for i in range(1, 8):
        other = 8 * z + lax.rem(y + i, 8)
        greet((other, 2 * x))
        greet((other, 2 * x + 1))
    for i in range(1, 8):
        greet((ctx, lax.rem(head + i, 8)))
    greet((lax.rem(ctx + 8, 64), head))
    greet((lax.rem(ctx + 56, 64), head))
    pl.when((c == 0) & (yh == 0))(lambda: greet((lax.rem(4 * group + 63, 64), 2 * x + 1)))

    @pl.when(c == 1)
    def _():
        for d in range(1, 5):
            greet((place(group - d, hl), head))

    rim_across = (c == 1) & (y == 7)

    for copy in inputs[8:]:
        copy.start()

    for copy in inputs[:8]:
        copy.wait()
    piece[...] = jnp.zeros((16, HD), BF16)
    for q in range(4):

        @pl.when(y % 4 == q)
        def _(q=q):
            piece[0:2, 32 * q : 32 * q + 32] = beta_w[0]
            piece[2:4, 32 * q : 32 * q + 32] = beta_w[1]

    pl.semaphore_wait(barrier, 23 + 4 * c + 4 * rim_across.astype(jnp.int32))

    mine_rows = pl.ds(pl.multiple_of(80 * (y // 2) + 32 * (y % 2), 16), 32)
    selfs = []
    for sub in range(2):
        local = 2 * c + sub
        for half in range(2):
            to = 8 * z + (local if half == 0 else 7 - local)
            me = to == ctx
            for core in range(2):
                device = (to, 2 * x + core)
                src = w_stage.at[0] if core == 0 else w_stage.at[1 + sub]
                is_self = me & (c == core)
                dst = w_mine.at[z, mine_rows, :]
                send(src, dst, y_sem.at[y], device, ~is_self)
                send(piece, pieces.at[y], p_sem.at[y], device, ~is_self)
                selfs.append((src, dst, is_self))
    for src, dst, is_self in selfs:

        @pl.when(is_self)
        def _(src=src, dst=dst):
            pltpu.make_async_copy(src, dst, y_sem.at[y]).start()
            pltpu.make_async_copy(piece, pieces.at[y], p_sem.at[y]).start()

    quarter = pl.ds(pl.multiple_of(32 * x, 32), 32)
    lanes = [pl.ds(1024 * i, 1024) for i in range(2)]
    rim_lanes = pl.ds(pl.multiple_of(512 * x, 512), 512)

    def tokens_out():
        owner = yl // 2 == c
        rows = pl.ds(pl.multiple_of(RIM + 128 * (yl % 2) + 32 * x, 16), 32)
        for i in range(2):
            for j in range(1, 4):
                to = 4 * group + lax.rem(yl + j, 4)
                dst = x_all.at[rows, lanes[i]]
                send(tokens.at[quarter, lanes[i]], dst, a1_sem.at[yl % 2, i], (to, head), owner)
        after_two = (c == 0) & (yl == 1)
        after_four = (c == 1) & (yl == 3)
        for j in range(4):
            last = tokens.at[pl.ds(128 - RIM, RIM), rim_lanes]
            to = jnp.where(after_two, 4 * group + j, lax.rem(4 * group + 4 + j, 64))
            dst = x_all.at[pl.ds(0, RIM), rim_lanes]
            send(last, dst, rim_sem.at[0], (to, 2 * x + 1 - c), after_two | after_four)

    for copy in inputs[8:]:
        copy.wait()
    for s in range(4):
        for i in range(2):
            p_mine[2 * s + i : 2 * s + i + 1, :] = conv_qk[s, i : i + 1, :]
        for i in range(2):
            p_mine[8 + 4 * i + s : 9 + 4 * i + s, :] = conv_value[s : s + 1, HD * i : HD * i + HD]
    for i in range(2):
        p_mine[16 + 2 * i : 17 + 2 * i, :] = jnp.full((1, HD), rate[i], F32)
        p_mine[17 + 2 * i : 18 + 2 * i, :] = jnp.full((1, HD), bias[i], F32)
    send(p_mine, p_other, par_sem, partner)
    own_block = []
    for k in range(2):
        is_own = yl == 2 * c + k
        block = x_all.at[pl.ds(RIM + 128 * k, 128), :]
        own_block.append((is_own, pltpu.make_async_copy(tokens, block, own_sem.at[0])))
        pl.when(is_own)(own_block[-1][1].start)
    own_out = pltpu.make_async_copy(
        w_out.at[:, pl.ds(pl.multiple_of(256 * head, 256), 256)],
        wo_all.at[pl.ds(pl.multiple_of(256 * head, 256), 256), :],
        own_sem.at[1],
    )
    own_out.start()

    base = 512 * group + 256 * c
    place_of = iota((256, HD), 0)
    start = jnp.full((256, HD), -FAR, jnp.int32)
    offset = -base
    for i in range(32):
        start = jnp.maximum(start, jnp.where(place_of >= offset, offset, -FAR))
        offset = offset + docs[i]

    ups, downs = lax.rem(ctx + 8, 64), lax.rem(ctx + 56, 64)
    parts = [lax.rem(y // 2 + i, 4) for i in (0, 1, 3, 2)]
    chunks = [pl.ds(pl.multiple_of(80 * part, 16), 64 if i < 3 else 80) for i, part in enumerate(parts)]
    narrow = [pl.ds(pl.multiple_of(80 * part, 16), 64) for part in parts]
    extra = pl.ds(pl.multiple_of(80 * parts[3] + 64, 16), 16)

    def onward(bundle, step, way, part):
        ref = w_mine.at[bundle, chunks[part], :]
        send(ref, ref, z_sem.at[way, step - 1, part], (ups if way == 0 else downs, head))

    def across(bundle, part):
        ref = narrow[part]
        send(w_mine.at[bundle, ref, :], w_other.at[bundle, ref, :], c_sem.at[bundle, part], partner)

    for part in range(4):
        for i in range(2):
            chip = 2 * parts[part] + i
            arrived(w_mine.at[z, pl.ds(pl.multiple_of(80 * parts[part] + 32 * i, 16), 32), :], y_sem.at[chip])
            arrived(pieces.at[chip], p_sem.at[chip])
        if part == 3:
            for i in range(2):
                joined = sum(pieces[4 * i + j].astype(F32) for j in range(4))
                w_mine[z, extra, HD * i : HD * i + HD] = joined.astype(BF16)
        onward(z, 1, 0, part)
        onward(z, 1, 1, part)
        if part == 0:
            tokens_out()
        across(z, part)

    def tokens_on(i):
        for k in range(2):
            is_remote = yl != 2 * c + k
            rows = pl.ds(pl.multiple_of(RIM + 128 * k + 32 * x, 16), 32)
            ref = x_all.at[rows, lanes[i]]
            pl.when(is_remote)(lambda ref=ref, k=k: arrived(ref, a1_sem.at[k, i]))
            for j in (1, 3, 2):
                send(ref, ref, a2_sem.at[k, j - 1, i], (ctx, 2 * lax.rem(x + j, 4) + c), is_remote)

    def rim_on():
        ref = x_all.at[pl.ds(0, RIM), rim_lanes]
        arrived(ref, rim_sem.at[0])
        for j in (1, 3, 2):
            send(ref, ref, rim_sem.at[j], (ctx, 2 * lax.rem(x + j, 4) + c))

    def all_tokens():
        for k in range(2):

            @pl.when(yl != 2 * c + k)
            def _(k=k):
                for i in range(2):
                    for j in range(1, 4):
                        rows = pl.ds(pl.multiple_of(RIM + 128 * k + 32 * lax.rem(x + 4 - j, 4), 16), 32)
                        arrived(x_all.at[rows, lanes[i]], a2_sem.at[k, j - 1, i])

            pl.when(own_block[k][0])(own_block[k][1].wait)
        for j in range(1, 4):
            there = pl.ds(pl.multiple_of(512 * lax.rem(x + 4 - j, 4), 512), 512)
            arrived(x_all.at[pl.ds(0, RIM), there], rim_sem.at[j])

    def multiply(bundle, first):
        rows = x_all[:, pl.ds(pl.multiple_of(256 * bundle, 256), 256)]

        def add(which, weights):
            product = dot(rows, jnp.concatenate([weights[bundle, 80 * i : 80 * i + 64, :] for i in range(4)], axis=0))
            acc[which] = product if first else acc[which] + product

        add(c, w_mine)
        small = dot(rows, w_mine[bundle, extra, :], ((1,), (1,)))
        logit[...] = small if first else logit[...] + small
        for part in range(4):
            arrived(w_other.at[bundle, narrow[part], :], c_sem.at[bundle, part])
        add(1 - c, w_other)

    tokens_on(0)
    for step in range(1, 5):
        below, above = lax.rem(z + 8 - step, 8), lax.rem(z + step, 8)
        for part in range(4):
            for way, bundle in ((0, below), (1, above)):
                if step == 4 and part // 2 != way:
                    continue
                arrived(w_mine.at[bundle, chunks[part], :], z_sem.at[way, step - 1, part])
                if step < 3 or (step == 3 and part // 2 == way):
                    onward(bundle, step + 1, way, part)
                across(bundle, part)
        if step == 1:
            tokens_on(1)
        if step == 1:
            rim_on()
        if step == 3:
            all_tokens()
            multiply(z, True)
            for near in range(1, 3):
                multiply(lax.rem(z + 8 - near, 8), False)
                multiply(lax.rem(z + near, 8), False)
        if step >= 3:
            multiply(below, False)
            if step < 4:
                multiply(above, False)

    for i in range(1, 8):
        to = lax.rem(head + i, 8)
        src = w_out.at[:, pl.ds(pl.multiple_of(256 * to, 256), 256)]
        dst = wo_all.at[pl.ds(pl.multiple_of(256 * head, 256), 256), :]
        send(src, dst, wo_sem.at[i - 1], (ctx, to))

    arrived(p_other, par_sem)
    settings = jnp.where(hl // 2 == c, p_mine[...], p_other[...])
    second = hl % 2 == 1
    acc[...] = acc[...].astype(BF16).astype(F32)

    def convolved(side, lanes, taps):
        total = acc[side, RIM : RIM + 256, lanes] * taps[3]
        for s in range(3):
            shifted = acc[side, RIM - 3 + s : RIM - 3 + s + 256, lanes]
            total = total + jnp.where(place_of - 3 + s >= start, shifted, 0.0) * taps[s]
        return total * sigmoid(total)

    def pick(low, high):
        return jnp.where(second, settings[high : high + 1], settings[low : low + 1])

    q_act = convolved(0, slice(0, HD), [settings[2 * s : 2 * s + 1] for s in range(4)])
    k_act = convolved(0, slice(HD, 2 * HD), [settings[2 * s + 1 : 2 * s + 2] for s in range(4)])
    v_act = convolved(1, slice(0, HD), [pick(8 + s, 12 + s) for s in range(4)])
    q_act = q_act * (lax.rsqrt(jnp.sum(q_act * q_act, axis=1, keepdims=True) + EPSILON) * HD**-0.5)
    k_act = k_act * lax.rsqrt(jnp.sum(k_act * k_act, axis=1, keepdims=True) + EPSILON)
    logits = logit[RIM:, :]
    beta_logit = jnp.where(second, logits[:, 1:2], logits[:, 0:1])
    decay_logit = jnp.where(second, logits[:, 3:4], logits[:, 2:3])
    beta = jnp.broadcast_to(sigmoid(beta_logit), (256, HD))
    shifted = jnp.broadcast_to(decay_logit, (256, HD)) + pick(17, 19)
    softplus = jnp.maximum(shifted, 0.0) + jnp.log1p(jnp.exp(-jnp.abs(shifted)))
    decay = -pick(16, 18) * softplus

    def blocks(array):
        return [array[:BLOCK], array[BLOCK:]]

    q_two, k_two, start_two = blocks(q_act), blocks(k_act), blocks(start)
    states, solved, ratio, lead = block_states(
        k_two, blocks(v_act), blocks(beta), blocks(decay), [start_two[0], start_two[1] - BLOCK]
    )
    z_unit[...] = compose(states[0], states[1])
    send(z_unit, z_first, zf_sem, partner, c == 0)

    targets = [(place(group + d, hl), head) for d in range(1, 5)]
    size = [2 * HD, 2 * HD, 2 * HD, HD]

    @pl.when(c == 1)
    def _():
        arrived(z_first, zf_sem)
        z_send[...] = compose(z_first[...], z_unit[...]).astype(BF16)

    for d in (2, 3, 0, 1):
        part = pl.ds(0, size[d])
        send(z_send.at[:, part], z_in.at[d, :, part], zi_sem.at[d], targets[d], c == 1)

    scores = each(lambda q, k, ratio: dot3(q, k.T) * ratio, q_two, k_two, ratio)
    mixed = each(dot3, scores, solved)
    leads = each(lambda q, lead, mixed: lead * q - mixed[:, HD:], q_two, lead, mixed)
    rests = each(lambda mixed: mixed[:, :HD], mixed)
    through = dot3(leads[1], states[0])
    leads[1], rests[1] = through[:, HD:], rests[1] + through[:, :HD]
    lead_all, rest_all = jnp.concatenate(leads, axis=0), jnp.concatenate(rests, axis=0)
    gate = acc[1, RIM:, HD:]
    gate = gate * sigmoid(gate) * gain[...]
    done = len(pending) - 5
    for copy, cond in pending[:done]:
        sent(copy, cond)

    @pl.when(c == 1)
    def _():
        for d in range(4):
            arrived(z_in.at[d, :, pl.ds(0, size[d])], zi_sem.at[d])
        state = z_in[3, :, :HD].astype(F32)
        for d in (2, 1, 0):
            state = dot2(z_in[d, :, HD:], state) + z_in[d, :, :HD].astype(F32)
        s_in[0] = state

    send(s_in.at[0], s_in.at[1], si_sem, partner, c == 1)
    pl.when(c == 0)(lambda: arrived(s_in.at[1], si_sem))

    @pl.when(c == 1)
    def _():
        s_in[1] = dot3(z_first[:, HD:], s_in[0]) + z_first[:, :HD]

    before = s_in[1]
    result = dot3(lead_all, before) + rest_all
    scale = lax.rsqrt(jnp.mean(result * result, axis=1, keepdims=True) + EPSILON)
    n_stage[...] = (result * scale * gate).astype(BF16)

    my_head = 4 * x + hl
    for b in range(2):
        src = n_stage.at[pl.ds(BLOCK * b, BLOCK), :]
        dst = n_all.at[my_head]
        is_self = (yl == 2 * c + b) & (hl % 2 == c)
        device = (4 * group + 2 * c + b, 2 * x + hl % 2)
        send(src, dst, n_sem.at[my_head], device, ~is_self)
        pl.when(is_self)(lambda src=src, dst=dst: pltpu.make_async_copy(src, dst, n_sem.at[my_head]).start())
    for m in range(2):
        which = 4 * x + 2 * m + c
        ref = n_all.at[which]
        arrived(ref, n_sem.at[which])
        for i in (1, 3, 2):
            send(ref, ref, n_sem.at[which], (ctx, 2 * lax.rem(x + i, 4) + c))
        send(ref, ref, n_sem.at[which], partner)
    for i in (1, 3, 2):
        for m in range(2):
            which = 4 * lax.rem(x + i, 4) + 2 * m + c
            ref = n_all.at[which]
            arrived(ref, n_sem.at[which])
            send(ref, ref, n_sem.at[which], partner)
    for i in range(1, 8):
        rows = pl.ds(pl.multiple_of(256 * lax.rem(head + 8 - i, 8), 256), 256)
        arrived(wo_all.at[rows, :], wo_sem.at[i - 1])
    own_out.wait()
    for i in range(8):
        which = 2 * i + 1 - c
        arrived(n_all.at[which], n_sem.at[which])
    total = jnp.zeros((128, 256), F32)
    for i in range(8):
        rows = jnp.concatenate([n_all[2 * i], n_all[2 * i + 1]], axis=1)
        total = total + dot(rows, wo_all[256 * i : 256 * i + 256, :])
    out[...] = total.astype(BF16)

    for copy, cond in pending[done:]:
        sent(copy, cond)


def local(
    tokens, w_query, w_key, w_value, w_output_gate, w_beta, w_decay, decay_rate, dt_bias, conv_qk, conv_value, norm_gain,
    w_out, doc_lengths,
):
    vmem = pl.BlockSpec(memory_space=pltpu.VMEM)
    dma = pltpu.SemaphoreType.DMA
    return pl.pallas_call(
        kernel,
        out_shape=jax.ShapeDtypeStruct((128, 256), BF16),
        in_specs=[pl.BlockSpec(memory_space=pltpu.HBM)] * 14,
        out_specs=vmem,
        scratch_shapes=[
            pltpu.VMEM((2, 2, 32), BF16),
            pltpu.SMEM((2,), F32),
            pltpu.SMEM((2,), F32),
            pltpu.VMEM((4, 2, HD), F32),
            pltpu.VMEM((4, 256), F32),
            pltpu.VMEM((1, HD), F32),
            pltpu.SMEM((32,), jnp.int32),
            pltpu.VMEM((RIM + 256, 2048), BF16),
            pltpu.VMEM((8, 320, 256), BF16),
            pltpu.VMEM((8, 320, 256), BF16),
            pltpu.VMEM((2048, 256), BF16),
            pltpu.VMEM((3, 32, 256), BF16),
            pltpu.VMEM((16, HD), BF16),
            pltpu.VMEM((8, 16, HD), BF16),
            pltpu.VMEM((24, HD), F32),
            pltpu.VMEM((24, HD), F32),
            pltpu.VMEM((2, RIM + 256, 256), F32),
            pltpu.VMEM((RIM + 256, 16), F32),
            pltpu.VMEM((HD, 2 * HD), F32),
            pltpu.VMEM((HD, 2 * HD), F32),
            pltpu.VMEM((HD, 2 * HD), BF16),
            pltpu.VMEM((4, HD, 2 * HD), BF16),
            pltpu.VMEM((2, HD, HD), F32),
            pltpu.VMEM((256, HD), BF16),
            pltpu.VMEM((16, 128, HD), BF16),
            dma((144,)),
            dma((2, 2)),
            dma((2, 3, 2)),
            dma((4,)),
            dma((8,)),
            dma((8,)),
            dma((2, 4, 4)),
            dma((8, 4)),
            dma((7,)),
            dma,
            dma,
            dma((4,)),
            dma,
            dma((16,)),
            dma((2,)),
            dma((14,)),
        ],
        compiler_params=pltpu.CompilerParams(
            collective_id=0, has_side_effects=True, vmem_limit_bytes=60 * 2**20
        ),
    )(
        tokens, w_query, w_key, w_value, w_output_gate, w_beta.T, w_decay.T, decay_rate, dt_bias, conv_qk, conv_value,
        norm_gain.reshape(1, HD), w_out, doc_lengths,
    )


def solution(mesh):
    return jax.shard_map(
        local,
        mesh=mesh,
        in_specs=(
            P("ctx", None),
            P("ctx", "head"),
            P("ctx", "head"),
            P("ctx", "head"),
            P("ctx", "head"),
            P("ctx", "head"),
            P("ctx", "head"),
            P("head"),
            P("head"),
            P(None, None, "head"),
            P(None, "head"),
            P(),
            P("head", None),
            P(),
        ),
        out_specs=P("ctx", "head"),
        check_vma=False,
    )
```

```python
import jax
import jax.numpy as jnp
from jax import lax
from jax.experimental import pallas as pl
from jax.experimental.pallas import tpu as pltpu
from jax.sharding import PartitionSpec as P

MESH = pl.DeviceIdType.MESH
EPSILON = 1e-06
HD = 128
BLOCK = 128
RIM = 16
F32 = jnp.float32
BF16 = jnp.bfloat16
FAR = 1 << 20


def dot(a, b, dims=((1,), (0,))):
    return lax.dot_general(a, b, (dims, ((), ())), preferred_element_type=F32)


def halves(a):
    high = a.astype(BF16)
    return high, (a - high.astype(F32)).astype(BF16)


def dot3(a, b):
    width = b.shape[1]
    (a_high, a_low), (b_high, b_low) = halves(a), halves(b)
    left = jnp.concatenate([a_high, a_low], axis=1)
    right = jnp.concatenate(
        [jnp.concatenate([b_high, b_low], axis=1), jnp.concatenate([b_high, jnp.zeros_like(b_low)], axis=1)], axis=0
    )
    both = dot(left, right)
    return both[:, :width] + both[:, width:]


def dot2(a, b):
    width = b.shape[1]
    both = dot(a, jnp.concatenate(halves(b), axis=1))
    return both[:, :width] + both[:, width:]


def iota(shape, dim):
    return lax.broadcasted_iota(jnp.int32, shape, dim)


def each(function, *lists):
    return [function(*items) for items in zip(*lists)]


def unit_lower_inverses(lowers):
    size = lowers[0].shape[0]
    row, col = iota((size, size), 0), iota((size, size), 1)
    inverses = each(lambda lower: jnp.where(row == col, 1.0, 0.0), lowers)
    shift = 0
    while (1 << shift) < size:
        joins = ((row >> (shift + 1)) == (col >> (shift + 1))) & ((row >> shift) != (col >> shift))
        parts = each(lambda lower: jnp.where(joins, lower, 0.0), lowers)
        if shift > 0:
            parts = each(dot3, each(dot3, inverses, parts), inverses)
        inverses = each(lambda inverse, part: inverse - part, inverses, parts)
        shift += 1
    return inverses


def block_states(k, v, beta, g, start):
    row, col = iota((BLOCK, BLOCK), 0), iota((BLOCK, BLOCK), 1)
    lower_tri = row >= col
    ones = jnp.where(lower_tri, 1.0, 0.0).astype(BF16)
    gam = each(lambda g: dot2(ones, g), g)
    inner = each(lambda k: dot3(k, k.T), k)
    ratio, lead, lower = [], [], []
    for b in range(len(k)):
        same = lower_tri & (col >= start[b])
        ratio.append(jnp.where(same, jnp.exp(jnp.where(same, gam[b] - gam[b].T, 0.0)), 0.0))
        lead.append(jnp.where(start[b] < 0, jnp.exp(gam[b]), 0.0))
        lower.append(jnp.where(row > col, beta[b] * ratio[b] * inner[b], 0.0))
    rights, lasts = [], []
    for b in range(len(k)):
        rights.append(jnp.concatenate([beta[b] * v[b], beta[b] * lead[b] * k[b]], axis=1))
        tail = jnp.where(row >= start[b][BLOCK - 1 :], jnp.exp(gam[b][BLOCK - 1 :] - gam[b]), 0.0)
        lasts.append((tail * k[b]).T)
    inverses = unit_lower_inverses(lower)
    solved = each(dot3, inverses, rights)
    joint = each(dot3, lasts, solved)
    states = []
    for b in range(len(k)):
        transition = jnp.where(row == col, lead[b][BLOCK - 1 :], 0.0) - joint[b][:, HD:]
        states.append(jnp.concatenate([joint[b][:, :HD], transition], axis=1))
    return states, solved, ratio, lead


def compose(earlier, later):
    joined = dot3(later[:, HD:], earlier)
    return jnp.concatenate([joined[:, :HD] + later[:, :HD], joined[:, HD:]], axis=1)


def sigmoid(x):
    return 1.0 / (1.0 + jnp.exp(-x))


def kernel(
    tokens, w_query, w_key, w_value, w_gate, w_beta, w_decay, rate_in, bias_in, conv_qk_in, conv_value_in, gain_in, w_out,
    docs_in,
    out,
    beta_w, rate, bias, conv_qk, conv_value, gain, docs,
    x_all, w_mine, w_other, wo_all, w_stage, piece, pieces, p_mine, p_other, acc, logit,
    z_unit, z_first, z_send, z_in, s_in, n_stage, n_all,
    send_sem, a1_sem, a2_sem, rim_sem, y_sem, p_sem, z_sem, c_sem, wo_sem, par_sem, zf_sem, zi_sem, si_sem, n_sem, own_sem,
    in_sem,
):
    ctx, head = lax.axis_index("ctx"), lax.axis_index("head")
    z, y = ctx // 8, ctx % 8
    x, c = head // 2, head % 2
    group, yl, yh = ctx // 4, ctx % 4, (ctx % 8) // 4
    hl = jnp.where(yh == 0, y, 7 - y)
    partner = (ctx, 2 * x + 1 - c)

    def place(g, local):
        g = lax.rem(g + 16, 16)
        return 8 * (g // 2) + jnp.where(g % 2 == 0, local, 7 - local)

    pending = []

    def send(src, dst, recv, device, cond=None):
        copy = pltpu.make_async_remote_copy(
            src_ref=src, dst_ref=dst, send_sem=send_sem.at[len(pending)], recv_sem=recv,
            device_id=device, device_id_type=MESH,
        )
        if cond is None:
            copy.start()
        else:
            pl.when(cond)(copy.start)
        pending.append((copy, cond))

    def sent(copy, cond):
        if cond is None:
            copy.wait_send()
        else:
            pl.when(cond)(copy.wait_send)

    def arrived(dst, sem):
        pltpu.make_async_copy(dst, dst, sem).wait()

    inputs = [
        pltpu.make_async_copy(src, dst, in_sem.at[i])
        for i, (src, dst) in enumerate(
            [
                (w_query, w_stage.at[0, :, :HD]),
                (w_key, w_stage.at[0, :, HD:]),
                (w_value.at[:, :HD], w_stage.at[1, :, :HD]),
                (w_value.at[:, HD:], w_stage.at[2, :, :HD]),
                (w_gate.at[:, :HD], w_stage.at[1, :, HD:]),
                (w_gate.at[:, HD:], w_stage.at[2, :, HD:]),
                (w_beta, beta_w.at[0]),
                (w_decay, beta_w.at[1]),
                (rate_in, rate),
                (bias_in, bias),
                (conv_qk_in, conv_qk),
                (conv_value_in, conv_value),
                (gain_in, gain),
                (docs_in, docs),
            ]
        )
    ]
    for copy in inputs[:8]:
        copy.start()

    barrier = pltpu.get_barrier_semaphore()

    def greet(device):
        pl.semaphore_signal(barrier, inc=1, device_id=device, device_id_type=MESH)

    for i in range(1, 8):
        other = 8 * z + lax.rem(y + i, 8)
        greet((other, 2 * x))
        greet((other, 2 * x + 1))
    for i in range(1, 8):
        greet((ctx, lax.rem(head + i, 8)))
    greet((lax.rem(ctx + 8, 64), head))
    greet((lax.rem(ctx + 56, 64), head))
    pl.when((c == 0) & (yh == 0))(lambda: greet((lax.rem(4 * group + 63, 64), 2 * x + 1)))

    @pl.when(c == 1)
    def _():
        for d in range(1, 5):
            greet((place(group - d, hl), head))

    rim_across = (c == 1) & (y == 7)

    for copy in inputs[8:]:
        copy.start()

    for copy in inputs[:8]:
        copy.wait()
    piece[...] = jnp.zeros((16, HD), BF16)
    for q in range(4):

        @pl.when(y % 4 == q)
        def _(q=q):
            piece[0:2, 32 * q : 32 * q + 32] = beta_w[0]
            piece[2:4, 32 * q : 32 * q + 32] = beta_w[1]

    pl.semaphore_wait(barrier, 23 + 4 * c + 4 * rim_across.astype(jnp.int32))

    mine_rows = pl.ds(pl.multiple_of(80 * (y // 2) + 32 * (y % 2), 16), 32)
    selfs = []
    for sub in range(2):
        local = 2 * c + sub
        for half in range(2):
            to = 8 * z + (local if half == 0 else 7 - local)
            me = to == ctx
            for core in range(2):
                device = (to, 2 * x + core)
                src = w_stage.at[0] if core == 0 else w_stage.at[1 + sub]
                is_self = me & (c == core)
                dst = w_mine.at[z, mine_rows, :]
                send(src, dst, y_sem.at[y], device, ~is_self)
                send(piece, pieces.at[y], p_sem.at[y], device, ~is_self)
                selfs.append((src, dst, is_self))
    for src, dst, is_self in selfs:

        @pl.when(is_self)
        def _(src=src, dst=dst):
            pltpu.make_async_copy(src, dst, y_sem.at[y]).start()
            pltpu.make_async_copy(piece, pieces.at[y], p_sem.at[y]).start()

    quarter = pl.ds(pl.multiple_of(32 * x, 32), 32)
    lanes = [pl.ds(1024 * i, 1024) for i in range(2)]
    rim_lanes = pl.ds(pl.multiple_of(512 * x, 512), 512)

    def tokens_out():
        owner = yl // 2 == c
        rows = pl.ds(pl.multiple_of(RIM + 128 * (yl % 2) + 32 * x, 16), 32)
        for i in range(2):
            for j in range(1, 4):
                to = 4 * group + lax.rem(yl + j, 4)
                dst = x_all.at[rows, lanes[i]]
                send(tokens.at[quarter, lanes[i]], dst, a1_sem.at[yl % 2, i], (to, head), owner)
        after_two = (c == 0) & (yl == 1)
        after_four = (c == 1) & (yl == 3)
        for j in range(4):
            last = tokens.at[pl.ds(128 - RIM, RIM), rim_lanes]
            to = jnp.where(after_two, 4 * group + j, lax.rem(4 * group + 4 + j, 64))
            dst = x_all.at[pl.ds(0, RIM), rim_lanes]
            send(last, dst, rim_sem.at[0], (to, 2 * x + 1 - c), after_two | after_four)

    for copy in inputs[8:]:
        copy.wait()
    for s in range(4):
        for i in range(2):
            p_mine[2 * s + i : 2 * s + i + 1, :] = conv_qk[s, i : i + 1, :]
        for i in range(2):
            p_mine[8 + 4 * i + s : 9 + 4 * i + s, :] = conv_value[s : s + 1, HD * i : HD * i + HD]
    for i in range(2):
        p_mine[16 + 2 * i : 17 + 2 * i, :] = jnp.full((1, HD), rate[i], F32)
        p_mine[17 + 2 * i : 18 + 2 * i, :] = jnp.full((1, HD), bias[i], F32)
    send(p_mine, p_other, par_sem, partner)
    own_block = []
    for k in range(2):
        is_own = yl == 2 * c + k
        block = x_all.at[pl.ds(RIM + 128 * k, 128), :]
        own_block.append((is_own, pltpu.make_async_copy(tokens, block, own_sem.at[0])))
        pl.when(is_own)(own_block[-1][1].start)
    own_out = pltpu.make_async_copy(
        w_out.at[:, pl.ds(pl.multiple_of(256 * head, 256), 256)],
        wo_all.at[pl.ds(pl.multiple_of(256 * head, 256), 256), :],
        own_sem.at[1],
    )
    own_out.start()

    base = 512 * group + 256 * c
    place_of = iota((256, HD), 0)
    start = jnp.full((256, HD), -FAR, jnp.int32)
    offset = -base
    for i in range(32):
        start = jnp.maximum(start, jnp.where(place_of >= offset, offset, -FAR))
        offset = offset + docs[i]

    ups, downs = lax.rem(ctx + 8, 64), lax.rem(ctx + 56, 64)
    parts = [lax.rem(y // 2 + i, 4) for i in (0, 1, 3, 2)]
    chunks = [pl.ds(pl.multiple_of(80 * part, 16), 64 if i < 3 else 80) for i, part in enumerate(parts)]
    narrow = [pl.ds(pl.multiple_of(80 * part, 16), 64) for part in parts]
    extra = pl.ds(pl.multiple_of(80 * parts[3] + 64, 16), 16)

    def onward(bundle, step, way, part):
        ref = w_mine.at[bundle, chunks[part], :]
        send(ref, ref, z_sem.at[way, step - 1, part], (ups if way == 0 else downs, head))

    def across(bundle, part):
        ref = narrow[part]
        send(w_mine.at[bundle, ref, :], w_other.at[bundle, ref, :], c_sem.at[bundle, part], partner)

    for part in range(4):
        for i in range(2):
            chip = 2 * parts[part] + i
            arrived(w_mine.at[z, pl.ds(pl.multiple_of(80 * parts[part] + 32 * i, 16), 32), :], y_sem.at[chip])
        if part == 3:
            for i in range(8):
                arrived(pieces.at[i], p_sem.at[i])
            for i in range(2):
                joined = sum(pieces[4 * i + j].astype(F32) for j in range(4))
                w_mine[z, extra, HD * i : HD * i + HD] = joined.astype(BF16)
        onward(z, 1, 0, part)
        onward(z, 1, 1, part)
        if part == 0:
            tokens_out()
        across(z, part)

    def tokens_on(i):
        for k in range(2):
            is_remote = yl != 2 * c + k
            rows = pl.ds(pl.multiple_of(RIM + 128 * k + 32 * x, 16), 32)
            ref = x_all.at[rows, lanes[i]]
            pl.when(is_remote)(lambda ref=ref, k=k: arrived(ref, a1_sem.at[k, i]))
            for j in (1, 3, 2):
                send(ref, ref, a2_sem.at[k, j - 1, i], (ctx, 2 * lax.rem(x + j, 4) + c), is_remote)

    def rim_on():
        ref = x_all.at[pl.ds(0, RIM), rim_lanes]
        arrived(ref, rim_sem.at[0])
        for j in (1, 3, 2):
            send(ref, ref, rim_sem.at[j], (ctx, 2 * lax.rem(x + j, 4) + c))

    def all_tokens():
        for k in range(2):

            @pl.when(yl != 2 * c + k)
            def _(k=k):
                for i in range(2):
                    for j in range(1, 4):
                        rows = pl.ds(pl.multiple_of(RIM + 128 * k + 32 * lax.rem(x + 4 - j, 4), 16), 32)
                        arrived(x_all.at[rows, lanes[i]], a2_sem.at[k, j - 1, i])

            pl.when(own_block[k][0])(own_block[k][1].wait)
        for j in range(1, 4):
            there = pl.ds(pl.multiple_of(512 * lax.rem(x + 4 - j, 4), 512), 512)
            arrived(x_all.at[pl.ds(0, RIM), there], rim_sem.at[j])

    def multiply(bundle, first):
        rows = x_all[:, pl.ds(pl.multiple_of(256 * bundle, 256), 256)]

        def add(which, weights):
            product = dot(rows, jnp.concatenate([weights[bundle, 80 * i : 80 * i + 64, :] for i in range(4)], axis=0))
            acc[which] = product if first else acc[which] + product

        add(c, w_mine)
        small = dot(rows, w_mine[bundle, extra, :], ((1,), (1,)))
        logit[...] = small if first else logit[...] + small
        for part in range(4):
            arrived(w_other.at[bundle, narrow[part], :], c_sem.at[bundle, part])
        add(1 - c, w_other)

    tokens_on(0)
    for step in range(1, 5):
        below, above = lax.rem(z + 8 - step, 8), lax.rem(z + step, 8)
        for part in range(4):
            for way, bundle in ((0, below), (1, above)):
                if step == 4 and part // 2 != way:
                    continue
                arrived(w_mine.at[bundle, chunks[part], :], z_sem.at[way, step - 1, part])
                if step < 3 or (step == 3 and part // 2 == way):
                    onward(bundle, step + 1, way, part)
                across(bundle, part)
        if step == 1:
            tokens_on(1)
        if step == 1:
            rim_on()
        if step == 3:
            all_tokens()
            multiply(z, True)
            for near in range(1, 3):
                multiply(lax.rem(z + 8 - near, 8), False)
                multiply(lax.rem(z + near, 8), False)
    for i in range(1, 8):
        to = lax.rem(head + i, 8)
        src = w_out.at[:, pl.ds(pl.multiple_of(256 * to, 256), 256)]
        dst = wo_all.at[pl.ds(pl.multiple_of(256 * head, 256), 256), :]
        send(src, dst, wo_sem.at[i - 1], (ctx, to))

    for near in range(3, 5):
        multiply(lax.rem(z + 8 - near, 8), False)
        if near < 4:
            multiply(lax.rem(z + near, 8), False)

    arrived(p_other, par_sem)
    settings = jnp.where(hl // 2 == c, p_mine[...], p_other[...])
    second = hl % 2 == 1
    acc[...] = acc[...].astype(BF16).astype(F32)

    def convolved(side, lanes, taps):
        total = acc[side, RIM : RIM + 256, lanes] * taps[3]
        for s in range(3):
            shifted = acc[side, RIM - 3 + s : RIM - 3 + s + 256, lanes]
            total = total + jnp.where(place_of - 3 + s >= start, shifted, 0.0) * taps[s]
        return total * sigmoid(total)

    def pick(low, high):
        return jnp.where(second, settings[high : high + 1], settings[low : low + 1])

    q_act = convolved(0, slice(0, HD), [settings[2 * s : 2 * s + 1] for s in range(4)])
    k_act = convolved(0, slice(HD, 2 * HD), [settings[2 * s + 1 : 2 * s + 2] for s in range(4)])
    v_act = convolved(1, slice(0, HD), [pick(8 + s, 12 + s) for s in range(4)])
    q_act = q_act * (lax.rsqrt(jnp.sum(q_act * q_act, axis=1, keepdims=True) + EPSILON) * HD**-0.5)
    k_act = k_act * lax.rsqrt(jnp.sum(k_act * k_act, axis=1, keepdims=True) + EPSILON)
    logits = logit[RIM:, :]
    beta_logit = jnp.where(second, logits[:, 1:2], logits[:, 0:1])
    decay_logit = jnp.where(second, logits[:, 3:4], logits[:, 2:3])
    beta = jnp.broadcast_to(sigmoid(beta_logit), (256, HD))
    shifted = jnp.broadcast_to(decay_logit, (256, HD)) + pick(17, 19)
    softplus = jnp.maximum(shifted, 0.0) + jnp.log1p(jnp.exp(-jnp.abs(shifted)))
    decay = -pick(16, 18) * softplus

    def blocks(array):
        return [array[:BLOCK], array[BLOCK:]]

    q_two, k_two, start_two = blocks(q_act), blocks(k_act), blocks(start)
    states, solved, ratio, lead = block_states(
        k_two, blocks(v_act), blocks(beta), blocks(decay), [start_two[0], start_two[1] - BLOCK]
    )
    z_unit[...] = compose(states[0], states[1])
    send(z_unit, z_first, zf_sem, partner, c == 0)

    targets = [(place(group + d, hl), head) for d in range(1, 5)]
    size = [2 * HD, 2 * HD, 2 * HD, HD]

    @pl.when(c == 1)
    def _():
        arrived(z_first, zf_sem)
        z_send[...] = compose(z_first[...], z_unit[...]).astype(BF16)

    for d in (2, 3, 0, 1):
        part = pl.ds(0, size[d])
        send(z_send.at[:, part], z_in.at[d, :, part], zi_sem.at[d], targets[d], c == 1)

    scores = each(lambda q, k, ratio: dot3(q, k.T) * ratio, q_two, k_two, ratio)
    mixed = each(dot3, scores, solved)
    leads = each(lambda q, lead, mixed: lead * q - mixed[:, HD:], q_two, lead, mixed)
    rests = each(lambda mixed: mixed[:, :HD], mixed)
    through = dot3(leads[1], states[0])
    leads[1], rests[1] = through[:, HD:], rests[1] + through[:, :HD]
    gate = acc[1, RIM:, HD:]
    gate = gate * sigmoid(gate) * gain[...]
    done = len(pending) - 5
    for copy, cond in pending[:done]:
        sent(copy, cond)

    @pl.when(c == 1)
    def _():
        for d in range(4):
            arrived(z_in.at[d, :, pl.ds(0, size[d])], zi_sem.at[d])
        state = z_in[3, :, :HD].astype(F32)
        for d in (2, 1, 0):
            state = dot2(z_in[d, :, HD:], state) + z_in[d, :, :HD].astype(F32)
        s_in[0] = state

    send(s_in.at[0], s_in.at[1], si_sem, partner, c == 1)
    pl.when(c == 0)(lambda: arrived(s_in.at[1], si_sem))

    @pl.when(c == 1)
    def _():
        s_in[1] = dot3(z_first[:, HD:], s_in[0]) + z_first[:, :HD]

    before = s_in[1]
    my_head = 4 * x + hl
    for b in range(2):
        rows = slice(BLOCK * b, BLOCK * b + BLOCK)
        result = dot3(leads[b], before) + rests[b]
        scale = lax.rsqrt(jnp.mean(result * result, axis=1, keepdims=True) + EPSILON)
        n_stage[rows, :] = (result * scale * gate[rows]).astype(BF16)
        src = n_stage.at[pl.ds(BLOCK * b, BLOCK), :]
        dst = n_all.at[my_head]
        is_self = (yl == 2 * c + b) & (hl % 2 == c)
        device = (4 * group + 2 * c + b, 2 * x + hl % 2)
        send(src, dst, n_sem.at[my_head], device, ~is_self)
        pl.when(is_self)(lambda src=src, dst=dst: pltpu.make_async_copy(src, dst, n_sem.at[my_head]).start())
    for m in range(2):
        which = 4 * x + 2 * m + c
        ref = n_all.at[which]
        arrived(ref, n_sem.at[which])
        for i in (1, 3, 2):
            send(ref, ref, n_sem.at[which], (ctx, 2 * lax.rem(x + i, 4) + c))
        send(ref, ref, n_sem.at[which], partner)
    for i in (1, 3, 2):
        for m in range(2):
            which = 4 * lax.rem(x + i, 4) + 2 * m + c
            ref = n_all.at[which]
            arrived(ref, n_sem.at[which])
            send(ref, ref, n_sem.at[which], partner)
    for i in range(1, 8):
        rows = pl.ds(pl.multiple_of(256 * lax.rem(head + 8 - i, 8), 256), 256)
        arrived(wo_all.at[rows, :], wo_sem.at[i - 1])
    own_out.wait()
    for i in range(8):
        which = 2 * i + 1 - c
        arrived(n_all.at[which], n_sem.at[which])
    total = jnp.zeros((128, 256), F32)
    for i in range(8):
        rows = jnp.concatenate([n_all[2 * i], n_all[2 * i + 1]], axis=1)
        total = total + dot(rows, wo_all[256 * i : 256 * i + 256, :])
    out[...] = total.astype(BF16)

    for copy, cond in pending[done:]:
        sent(copy, cond)


def local(
    tokens, w_query, w_key, w_value, w_output_gate, w_beta, w_decay, decay_rate, dt_bias, conv_qk, conv_value, norm_gain,
    w_out, doc_lengths,
):
    vmem = pl.BlockSpec(memory_space=pltpu.VMEM)
    dma = pltpu.SemaphoreType.DMA
    return pl.pallas_call(
        kernel,
        out_shape=pltpu.VMEM((128, 256), BF16),
        in_specs=[pl.BlockSpec(memory_space=pltpu.HBM)] * 14,
        out_specs=vmem,
        scratch_shapes=[
            pltpu.VMEM((2, 2, 32), BF16),
            pltpu.SMEM((2,), F32),
            pltpu.SMEM((2,), F32),
            pltpu.VMEM((4, 2, HD), F32),
            pltpu.VMEM((4, 256), F32),
            pltpu.VMEM((1, HD), F32),
            pltpu.SMEM((32,), jnp.int32),
            pltpu.VMEM((RIM + 256, 2048), BF16),
            pltpu.VMEM((8, 320, 256), BF16),
            pltpu.VMEM((8, 320, 256), BF16),
            pltpu.VMEM((2048, 256), BF16),
            pltpu.VMEM((3, 32, 256), BF16),
            pltpu.VMEM((16, HD), BF16),
            pltpu.VMEM((8, 16, HD), BF16),
            pltpu.VMEM((24, HD), F32),
            pltpu.VMEM((24, HD), F32),
            pltpu.VMEM((2, RIM + 256, 256), F32),
            pltpu.VMEM((RIM + 256, 16), F32),
            pltpu.VMEM((HD, 2 * HD), F32),
            pltpu.VMEM((HD, 2 * HD), F32),
            pltpu.VMEM((HD, 2 * HD), BF16),
            pltpu.VMEM((4, HD, 2 * HD), BF16),
            pltpu.VMEM((2, HD, HD), F32),
            pltpu.VMEM((256, HD), BF16),
            pltpu.VMEM((16, 128, HD), BF16),
            dma((144,)),
            dma((2, 2)),
            dma((2, 3, 2)),
            dma((4,)),
            dma((8,)),
            dma((8,)),
            dma((2, 4, 4)),
            dma((8, 4)),
            dma((7,)),
            dma,
            dma,
            dma((4,)),
            dma,
            dma((16,)),
            dma((2,)),
            dma((14,)),
        ],
        compiler_params=pltpu.CompilerParams(
            collective_id=0, has_side_effects=True, vmem_limit_bytes=60 * 2**20
        ),
    )(
        tokens, w_query, w_key, w_value, w_output_gate, w_beta.T, w_decay.T, decay_rate, dt_bias, conv_qk, conv_value,
        norm_gain.reshape(1, HD), w_out, doc_lengths,
    )


def solution(mesh):
    return jax.shard_map(
        local,
        mesh=mesh,
        in_specs=(
            P("ctx", None),
            P("ctx", "head"),
            P("ctx", "head"),
            P("ctx", "head"),
            P("ctx", "head"),
            P("ctx", "head"),
            P("ctx", "head"),
            P("head"),
            P("head"),
            P(None, None, "head"),
            P(None, "head"),
            P(),
            P("head", None),
            P(),
        ),
        out_specs=P("ctx", "head"),
        check_vma=False,
    )
```

```python
import jax
import jax.numpy as jnp
from jax import lax
from jax.experimental import pallas as pl
from jax.experimental.pallas import tpu as pltpu
from jax.sharding import PartitionSpec as P

MESH = pl.DeviceIdType.MESH
EPSILON = 1e-06
HD = 128
BLOCK = 128
RIM = 16
F32 = jnp.float32
BF16 = jnp.bfloat16
FAR = 1 << 20


def dot(a, b, dims=((1,), (0,))):
    return lax.dot_general(a, b, (dims, ((), ())), preferred_element_type=F32)


def halves(a):
    high = a.astype(BF16)
    return high, (a - high.astype(F32)).astype(BF16)


def dot3(a, b):
    width = b.shape[1]
    (a_high, a_low), (b_high, b_low) = halves(a), halves(b)
    left = jnp.concatenate([a_high, a_low], axis=1)
    right = jnp.concatenate(
        [jnp.concatenate([b_high, b_low], axis=1), jnp.concatenate([b_high, jnp.zeros_like(b_low)], axis=1)], axis=0
    )
    both = dot(left, right)
    return both[:, :width] + both[:, width:]


def dot2(a, b):
    width = b.shape[1]
    both = dot(a, jnp.concatenate(halves(b), axis=1))
    return both[:, :width] + both[:, width:]


def iota(shape, dim):
    return lax.broadcasted_iota(jnp.int32, shape, dim)


def each(function, *lists):
    return [function(*items) for items in zip(*lists)]


def unit_lower_inverses(lowers):
    size = lowers[0].shape[0]
    row, col = iota((size, size), 0), iota((size, size), 1)
    inverses = each(lambda lower: jnp.where(row == col, 1.0, 0.0), lowers)
    shift = 0
    while (1 << shift) < size:
        joins = ((row >> (shift + 1)) == (col >> (shift + 1))) & ((row >> shift) != (col >> shift))
        parts = each(lambda lower: jnp.where(joins, lower, 0.0), lowers)
        if shift > 0:
            parts = each(dot3, each(dot3, inverses, parts), inverses)
        inverses = each(lambda inverse, part: inverse - part, inverses, parts)
        shift += 1
    return inverses


def block_states(k, v, beta, g, start):
    row, col = iota((BLOCK, BLOCK), 0), iota((BLOCK, BLOCK), 1)
    lower_tri = row >= col
    ones = jnp.where(lower_tri, 1.0, 0.0).astype(BF16)
    gam = each(lambda g: dot2(ones, g), g)
    inner = each(lambda k: dot3(k, k.T), k)
    ratio, lead, lower = [], [], []
    for b in range(len(k)):
        same = lower_tri & (col >= start[b])
        ratio.append(jnp.where(same, jnp.exp(jnp.where(same, gam[b] - gam[b].T, 0.0)), 0.0))
        lead.append(jnp.where(start[b] < 0, jnp.exp(gam[b]), 0.0))
        lower.append(jnp.where(row > col, beta[b] * ratio[b] * inner[b], 0.0))
    rights, lasts = [], []
    for b in range(len(k)):
        rights.append(jnp.concatenate([beta[b] * v[b], beta[b] * lead[b] * k[b]], axis=1))
        tail = jnp.where(row >= start[b][BLOCK - 1 :], jnp.exp(gam[b][BLOCK - 1 :] - gam[b]), 0.0)
        lasts.append((tail * k[b]).T)
    inverses = unit_lower_inverses(lower)
    solved = each(dot3, inverses, rights)
    joint = each(dot3, lasts, solved)
    states = []
    for b in range(len(k)):
        transition = jnp.where(row == col, lead[b][BLOCK - 1 :], 0.0) - joint[b][:, HD:]
        states.append(jnp.concatenate([joint[b][:, :HD], transition], axis=1))
    return states, solved, ratio, lead


def compose(earlier, later):
    joined = dot3(later[:, HD:], earlier)
    return jnp.concatenate([joined[:, :HD] + later[:, :HD], joined[:, HD:]], axis=1)


def sigmoid(x):
    return 1.0 / (1.0 + jnp.exp(-x))


def kernel(
    tokens, w_query, w_key, w_value, w_gate, w_small, rate_in, bias_in, conv_qk_in, conv_value_in, gain_in, w_out,
    docs_in,
    out,
    small_w, rate, bias, conv_qk, conv_value, gain, docs,
    x_all, w_mine, w_other, wo_all, w_stage, piece, pieces, p_mine, p_other, acc, logit,
    z_unit, z_first, z_send, z_in, s_in, n_stage, n_all,
    send_sem, a1_sem, a2_sem, rim_sem, y_sem, p_sem, z_sem, c_sem, wo_sem, par_sem, zf_sem, zi_sem, si_sem, n_sem, own_sem,
    in_sem,
):
    ctx, head = lax.axis_index("ctx"), lax.axis_index("head")
    z, y = ctx // 8, ctx % 8
    x, c = head // 2, head % 2
    group, yl, yh = ctx // 4, ctx % 4, (ctx % 8) // 4
    hl = jnp.where(yh == 0, y, 7 - y)
    partner = (ctx, 2 * x + 1 - c)

    def place(g, local):
        g = lax.rem(g + 16, 16)
        return 8 * (g // 2) + jnp.where(g % 2 == 0, local, 7 - local)

    pending = []

    def send(src, dst, recv, device, cond=None):
        copy = pltpu.make_async_remote_copy(
            src_ref=src, dst_ref=dst, send_sem=send_sem.at[len(pending)], recv_sem=recv,
            device_id=device, device_id_type=MESH,
        )
        if cond is None:
            copy.start()
        else:
            pl.when(cond)(copy.start)
        pending.append((copy, cond))

    def sent(copy, cond):
        if cond is None:
            copy.wait_send()
        else:
            pl.when(cond)(copy.wait_send)

    def arrived(dst, sem):
        pltpu.make_async_copy(dst, dst, sem).wait()

    inputs = [
        pltpu.make_async_copy(src, dst, in_sem.at[i])
        for i, (src, dst) in enumerate(
            [
                (w_query, w_stage.at[0, :, :HD]),
                (w_key, w_stage.at[0, :, HD:]),
                (w_value.at[:, :HD], w_stage.at[1, :, :HD]),
                (w_value.at[:, HD:], w_stage.at[2, :, :HD]),
                (w_gate.at[:, :HD], w_stage.at[1, :, HD:]),
                (w_gate.at[:, HD:], w_stage.at[2, :, HD:]),
                (w_small, small_w),
                (rate_in, rate),
                (bias_in, bias),
                (conv_qk_in, conv_qk),
                (conv_value_in, conv_value),
                (gain_in, gain),
                (docs_in, docs),
            ]
        )
    ]
    for copy in inputs[:7]:
        copy.start()

    barrier = pltpu.get_barrier_semaphore()

    def greet(device):
        pl.semaphore_signal(barrier, inc=1, device_id=device, device_id_type=MESH)

    for i in range(1, 8):
        other = 8 * z + lax.rem(y + i, 8)
        greet((other, 2 * x))
        greet((other, 2 * x + 1))
    for i in range(1, 8):
        greet((ctx, lax.rem(head + i, 8)))
    greet((lax.rem(ctx + 8, 64), head))
    greet((lax.rem(ctx + 56, 64), head))
    pl.when((c == 0) & (yh == 0))(lambda: greet((lax.rem(4 * group + 63, 64), 2 * x + 1)))

    @pl.when(c == 1)
    def _():
        for d in range(1, 5):
            greet((place(group - d, hl), head))

    rim_across = (c == 1) & (y == 7)

    for copy in inputs[7:]:
        copy.start()

    for copy in inputs[:7]:
        copy.wait()
    piece[...] = jnp.zeros((16, HD), BF16)
    for q in range(4):

        @pl.when(y % 4 == q)
        def _(q=q):
            piece[0:4, 32 * q : 32 * q + 32] = small_w[...].astype(BF16)

    pl.semaphore_wait(barrier, 23 + 4 * c + 4 * rim_across.astype(jnp.int32))

    mine_rows = pl.ds(pl.multiple_of(80 * (y // 2) + 32 * (y % 2), 16), 32)
    selfs = []
    for sub in range(2):
        local = 2 * c + sub
        for half in range(2):
            to = 8 * z + (local if half == 0 else 7 - local)
            me = to == ctx
            for core in range(2):
                device = (to, 2 * x + core)
                src = w_stage.at[0] if core == 0 else w_stage.at[1 + sub]
                is_self = me & (c == core)
                dst = w_mine.at[z, mine_rows, :]
                send(src, dst, y_sem.at[y], device, ~is_self)
                send(piece, pieces.at[y], p_sem.at[y], device, ~is_self)
                selfs.append((src, dst, is_self))
    for src, dst, is_self in selfs:

        @pl.when(is_self)
        def _(src=src, dst=dst):
            pltpu.make_async_copy(src, dst, y_sem.at[y]).start()
            pltpu.make_async_copy(piece, pieces.at[y], p_sem.at[y]).start()

    quarter = pl.ds(pl.multiple_of(32 * x, 32), 32)
    lanes = [pl.ds(1024 * i, 1024) for i in range(2)]
    rim_lanes = pl.ds(pl.multiple_of(512 * x, 512), 512)

    def tokens_out():
        owner = yl // 2 == c
        rows = pl.ds(pl.multiple_of(RIM + 128 * (yl % 2) + 32 * x, 16), 32)
        for i in range(2):
            for j in range(1, 4):
                to = 4 * group + lax.rem(yl + j, 4)
                dst = x_all.at[rows, lanes[i]]
                send(tokens.at[quarter, lanes[i]], dst, a1_sem.at[yl % 2, i], (to, head), owner)
        after_two = (c == 0) & (yl == 1)
        after_four = (c == 1) & (yl == 3)
        for j in range(4):
            last = tokens.at[pl.ds(128 - RIM, RIM), rim_lanes]
            to = jnp.where(after_two, 4 * group + j, lax.rem(4 * group + 4 + j, 64))
            dst = x_all.at[pl.ds(0, RIM), rim_lanes]
            send(last, dst, rim_sem.at[0], (to, 2 * x + 1 - c), after_two | after_four)

    for copy in inputs[7:]:
        copy.wait()
    for s in range(4):
        for i in range(2):
            p_mine[2 * s + i : 2 * s + i + 1, :] = conv_qk[s, i : i + 1, :]
        for i in range(2):
            p_mine[8 + 4 * i + s : 9 + 4 * i + s, :] = conv_value[s : s + 1, HD * i : HD * i + HD]
    for i in range(2):
        p_mine[16 + 2 * i : 17 + 2 * i, :] = jnp.full((1, HD), rate[i], F32)
        p_mine[17 + 2 * i : 18 + 2 * i, :] = jnp.full((1, HD), bias[i], F32)
    send(p_mine, p_other, par_sem, partner)
    own_block = []
    for k in range(2):
        is_own = yl == 2 * c + k
        block = x_all.at[pl.ds(RIM + 128 * k, 128), :]
        own_block.append((is_own, pltpu.make_async_copy(tokens, block, own_sem.at[0])))
        pl.when(is_own)(own_block[-1][1].start)
    own_out = pltpu.make_async_copy(
        w_out.at[:, pl.ds(pl.multiple_of(256 * head, 256), 256)],
        wo_all.at[pl.ds(pl.multiple_of(256 * head, 256), 256), :],
        own_sem.at[1],
    )
    own_out.start()

    base = 512 * group + 256 * c
    place_of = iota((256, HD), 0)
    start = jnp.full((256, HD), -FAR, jnp.int32)
    offset = -base
    for i in range(32):
        start = jnp.maximum(start, jnp.where(place_of >= offset, offset, -FAR))
        offset = offset + docs[i]

    ups, downs = lax.rem(ctx + 8, 64), lax.rem(ctx + 56, 64)
    parts = [lax.rem(y // 2 + i, 4) for i in (0, 1, 3, 2)]
    chunks = [pl.ds(pl.multiple_of(80 * part, 16), 64 if i < 3 else 80) for i, part in enumerate(parts)]
    narrow = [pl.ds(pl.multiple_of(80 * part, 16), 64) for part in parts]
    extra = pl.ds(pl.multiple_of(80 * parts[3] + 64, 16), 16)

    def onward(bundle, step, way, part):
        ref = w_mine.at[bundle, chunks[part], :]
        send(ref, ref, z_sem.at[way, step - 1, part], (ups if way == 0 else downs, head))

    def across(bundle, part):
        ref = narrow[part]
        send(w_mine.at[bundle, ref, :], w_other.at[bundle, ref, :], c_sem.at[bundle, part], partner)

    for part in range(4):
        for i in range(2):
            chip = 2 * parts[part] + i
            arrived(w_mine.at[z, pl.ds(pl.multiple_of(80 * parts[part] + 32 * i, 16), 32), :], y_sem.at[chip])
        if part == 3:
            for i in range(8):
                arrived(pieces.at[i], p_sem.at[i])
            for i in range(2):
                joined = sum(pieces[4 * i + j].astype(F32) for j in range(4))
                w_mine[z, extra, HD * i : HD * i + HD] = joined.astype(BF16)
        onward(z, 1, 0, part)
        onward(z, 1, 1, part)
        if part == 0:
            tokens_out()
        across(z, part)

    def tokens_on(i):
        for k in range(2):
            is_remote = yl != 2 * c + k
            rows = pl.ds(pl.multiple_of(RIM + 128 * k + 32 * x, 16), 32)
            ref = x_all.at[rows, lanes[i]]
            pl.when(is_remote)(lambda ref=ref, k=k: arrived(ref, a1_sem.at[k, i]))
            for j in (1, 3, 2):
                send(ref, ref, a2_sem.at[k, j - 1, i], (ctx, 2 * lax.rem(x + j, 4) + c), is_remote)

    def rim_on():
        ref = x_all.at[pl.ds(0, RIM), rim_lanes]
        arrived(ref, rim_sem.at[0])
        for j in (1, 3, 2):
            send(ref, ref, rim_sem.at[j], (ctx, 2 * lax.rem(x + j, 4) + c))

    def all_tokens():
        for k in range(2):

            @pl.when(yl != 2 * c + k)
            def _(k=k):
                for i in range(2):
                    for j in range(1, 4):
                        rows = pl.ds(pl.multiple_of(RIM + 128 * k + 32 * lax.rem(x + 4 - j, 4), 16), 32)
                        arrived(x_all.at[rows, lanes[i]], a2_sem.at[k, j - 1, i])

            pl.when(own_block[k][0])(own_block[k][1].wait)
        for j in range(1, 4):
            there = pl.ds(pl.multiple_of(512 * lax.rem(x + 4 - j, 4), 512), 512)
            arrived(x_all.at[pl.ds(0, RIM), there], rim_sem.at[j])

    def multiply(bundle, first):
        rows = x_all[:, pl.ds(pl.multiple_of(256 * bundle, 256), 256)]

        def add(which, weights):
            product = dot(rows, jnp.concatenate([weights[bundle, 80 * i : 80 * i + 64, :] for i in range(4)], axis=0))
            acc[which] = product if first else acc[which] + product

        add(c, w_mine)
        small = dot(rows, w_mine[bundle, extra, :], ((1,), (1,)))
        logit[...] = small if first else logit[...] + small
        for part in range(4):
            arrived(w_other.at[bundle, narrow[part], :], c_sem.at[bundle, part])
        add(1 - c, w_other)

    tokens_on(0)
    for step in range(1, 5):
        below, above = lax.rem(z + 8 - step, 8), lax.rem(z + step, 8)
        for part in range(4):
            for way, bundle in ((0, below), (1, above)):
                if step == 4 and part // 2 != way:
                    continue
                arrived(w_mine.at[bundle, chunks[part], :], z_sem.at[way, step - 1, part])
                if step < 3 or (step == 3 and part // 2 == way):
                    onward(bundle, step + 1, way, part)
                across(bundle, part)
        if step == 1:
            tokens_on(1)
        if step == 1:
            rim_on()
        if step == 3:
            all_tokens()
            multiply(z, True)
            for near in range(1, 3):
                multiply(lax.rem(z + 8 - near, 8), False)
                multiply(lax.rem(z + near, 8), False)
    for i in range(1, 8):
        to = lax.rem(head + i, 8)
        src = w_out.at[:, pl.ds(pl.multiple_of(256 * to, 256), 256)]
        dst = wo_all.at[pl.ds(pl.multiple_of(256 * head, 256), 256), :]
        send(src, dst, wo_sem.at[i - 1], (ctx, to))

    for near in range(3, 5):
        multiply(lax.rem(z + 8 - near, 8), False)
        if near < 4:
            multiply(lax.rem(z + near, 8), False)

    arrived(p_other, par_sem)
    settings = jnp.where(hl // 2 == c, p_mine[...], p_other[...])
    second = hl % 2 == 1
    acc[...] = acc[...].astype(BF16).astype(F32)

    def convolved(side, lanes, taps):
        total = acc[side, RIM : RIM + 256, lanes] * taps[3]
        for s in range(3):
            shifted = acc[side, RIM - 3 + s : RIM - 3 + s + 256, lanes]
            total = total + jnp.where(place_of - 3 + s >= start, shifted, 0.0) * taps[s]
        return total * sigmoid(total)

    def pick(low, high):
        return jnp.where(second, settings[high : high + 1], settings[low : low + 1])

    q_act = convolved(0, slice(0, HD), [settings[2 * s : 2 * s + 1] for s in range(4)])
    k_act = convolved(0, slice(HD, 2 * HD), [settings[2 * s + 1 : 2 * s + 2] for s in range(4)])
    v_act = convolved(1, slice(0, HD), [pick(8 + s, 12 + s) for s in range(4)])
    q_act = q_act * (lax.rsqrt(jnp.sum(q_act * q_act, axis=1, keepdims=True) + EPSILON) * HD**-0.5)
    k_act = k_act * lax.rsqrt(jnp.sum(k_act * k_act, axis=1, keepdims=True) + EPSILON)
    logits = logit[RIM:, :]
    beta_logit = jnp.where(second, logits[:, 1:2], logits[:, 0:1])
    decay_logit = jnp.where(second, logits[:, 3:4], logits[:, 2:3])
    beta = jnp.broadcast_to(sigmoid(beta_logit), (256, HD))
    shifted = jnp.broadcast_to(decay_logit, (256, HD)) + pick(17, 19)
    softplus = jnp.maximum(shifted, 0.0) + jnp.log1p(jnp.exp(-jnp.abs(shifted)))
    decay = -pick(16, 18) * softplus

    def blocks(array):
        return [array[:BLOCK], array[BLOCK:]]

    q_two, k_two, start_two = blocks(q_act), blocks(k_act), blocks(start)
    states, solved, ratio, lead = block_states(
        k_two, blocks(v_act), blocks(beta), blocks(decay), [start_two[0], start_two[1] - BLOCK]
    )
    z_unit[...] = compose(states[0], states[1])
    send(z_unit, z_first, zf_sem, partner, c == 0)

    targets = [(place(group + d, hl), head) for d in range(1, 5)]
    size = [2 * HD, 2 * HD, 2 * HD, HD]

    @pl.when(c == 1)
    def _():
        arrived(z_first, zf_sem)
        z_send[...] = compose(z_first[...], z_unit[...]).astype(BF16)

    for d in (2, 3, 0, 1):
        part = pl.ds(0, size[d])
        send(z_send.at[:, part], z_in.at[d, :, part], zi_sem.at[d], targets[d], c == 1)

    scores = each(lambda q, k, ratio: dot3(q, k.T) * ratio, q_two, k_two, ratio)
    mixed = each(dot3, scores, solved)
    leads = each(lambda q, lead, mixed: lead * q - mixed[:, HD:], q_two, lead, mixed)
    rests = each(lambda mixed: mixed[:, :HD], mixed)
    through = dot3(leads[1], states[0])
    leads[1], rests[1] = through[:, HD:], rests[1] + through[:, :HD]
    gate = acc[1, RIM:, HD:]
    gate = gate * sigmoid(gate) * gain[...]
    done = len(pending) - 5
    for copy, cond in pending[:done]:
        sent(copy, cond)

    @pl.when(c == 1)
    def _():
        for d in range(4):
            arrived(z_in.at[d, :, pl.ds(0, size[d])], zi_sem.at[d])
        state = z_in[3, :, :HD].astype(F32)
        for d in (2, 1, 0):
            state = dot2(z_in[d, :, HD:], state) + z_in[d, :, :HD].astype(F32)
        s_in[0] = state

    send(s_in.at[0], s_in.at[1], si_sem, partner, c == 1)
    pl.when(c == 0)(lambda: arrived(s_in.at[1], si_sem))

    @pl.when(c == 1)
    def _():
        s_in[1] = dot3(z_first[:, HD:], s_in[0]) + z_first[:, :HD]

    before = s_in[1]
    my_head = 4 * x + hl
    for b in range(2):
        rows = slice(BLOCK * b, BLOCK * b + BLOCK)
        result = dot3(leads[b], before) + rests[b]
        scale = lax.rsqrt(jnp.mean(result * result, axis=1, keepdims=True) + EPSILON)
        n_stage[rows, :] = (result * scale * gate[rows]).astype(BF16)
        src = n_stage.at[pl.ds(BLOCK * b, BLOCK), :]
        dst = n_all.at[my_head]
        is_self = (yl == 2 * c + b) & (hl % 2 == c)
        device = (4 * group + 2 * c + b, 2 * x + hl % 2)
        send(src, dst, n_sem.at[my_head], device, ~is_self)
        pl.when(is_self)(lambda src=src, dst=dst: pltpu.make_async_copy(src, dst, n_sem.at[my_head]).start())
    for m in range(2):
        which = 4 * x + 2 * m + c
        ref = n_all.at[which]
        arrived(ref, n_sem.at[which])
        for i in (1, 3, 2):
            send(ref, ref, n_sem.at[which], (ctx, 2 * lax.rem(x + i, 4) + c))
        send(ref, ref, n_sem.at[which], partner)
    for i in (1, 3, 2):
        for m in range(2):
            which = 4 * lax.rem(x + i, 4) + 2 * m + c
            ref = n_all.at[which]
            arrived(ref, n_sem.at[which])
            send(ref, ref, n_sem.at[which], partner)
    for i in range(1, 8):
        rows = pl.ds(pl.multiple_of(256 * lax.rem(head + 8 - i, 8), 256), 256)
        arrived(wo_all.at[rows, :], wo_sem.at[i - 1])
    own_out.wait()
    for i in range(8):
        which = 2 * i + 1 - c
        arrived(n_all.at[which], n_sem.at[which])
    total = jnp.zeros((128, 256), F32)
    for i in range(8):
        rows = jnp.concatenate([n_all[2 * i], n_all[2 * i + 1]], axis=1)
        total = total + dot(rows, wo_all[256 * i : 256 * i + 256, :])
    out[...] = total.astype(BF16)

    for copy, cond in pending[done:]:
        sent(copy, cond)


def local(
    tokens, w_query, w_key, w_value, w_output_gate, w_beta, w_decay, decay_rate, dt_bias, conv_qk, conv_value, norm_gain,
    w_out, doc_lengths,
):
    vmem = pl.BlockSpec(memory_space=pltpu.VMEM)
    small = jnp.concatenate([w_beta.T, w_decay.T], axis=0).astype(F32)
    dma = pltpu.SemaphoreType.DMA
    return pl.pallas_call(
        kernel,
        out_shape=pltpu.VMEM((128, 256), BF16),
        in_specs=[pl.BlockSpec(memory_space=pltpu.HBM)] * 13,
        out_specs=vmem,
        scratch_shapes=[
            pltpu.VMEM((4, 32), F32),
            pltpu.SMEM((2,), F32),
            pltpu.SMEM((2,), F32),
            pltpu.VMEM((4, 2, HD), F32),
            pltpu.VMEM((4, 256), F32),
            pltpu.VMEM((1, HD), F32),
            pltpu.SMEM((32,), jnp.int32),
            pltpu.VMEM((RIM + 256, 2048), BF16),
            pltpu.VMEM((8, 320, 256), BF16),
            pltpu.VMEM((8, 320, 256), BF16),
            pltpu.VMEM((2048, 256), BF16),
            pltpu.VMEM((3, 32, 256), BF16),
            pltpu.VMEM((16, HD), BF16),
            pltpu.VMEM((8, 16, HD), BF16),
            pltpu.VMEM((24, HD), F32),
            pltpu.VMEM((24, HD), F32),
            pltpu.VMEM((2, RIM + 256, 256), F32),
            pltpu.VMEM((RIM + 256, 16), F32),
            pltpu.VMEM((HD, 2 * HD), F32),
            pltpu.VMEM((HD, 2 * HD), F32),
            pltpu.VMEM((HD, 2 * HD), BF16),
            pltpu.VMEM((4, HD, 2 * HD), BF16),
            pltpu.VMEM((2, HD, HD), F32),
            pltpu.VMEM((256, HD), BF16),
            pltpu.VMEM((16, 128, HD), BF16),
            dma((144,)),
            dma((2, 2)),
            dma((2, 3, 2)),
            dma((4,)),
            dma((8,)),
            dma((8,)),
            dma((2, 4, 4)),
            dma((8, 4)),
            dma((7,)),
            dma,
            dma,
            dma((4,)),
            dma,
            dma((16,)),
            dma((2,)),
            dma((13,)),
        ],
        compiler_params=pltpu.CompilerParams(
            collective_id=0, has_side_effects=True, vmem_limit_bytes=60 * 2**20
        ),
    )(
        tokens, w_query, w_key, w_value, w_output_gate, small, decay_rate, dt_bias, conv_qk, conv_value,
        norm_gain.reshape(1, HD), w_out, doc_lengths,
    )


def solution(mesh):
    return jax.shard_map(
        local,
        mesh=mesh,
        in_specs=(
            P("ctx", None),
            P("ctx", "head"),
            P("ctx", "head"),
            P("ctx", "head"),
            P("ctx", "head"),
            P("ctx", "head"),
            P("ctx", "head"),
            P("head"),
            P("head"),
            P(None, None, "head"),
            P(None, "head"),
            P(),
            P("head", None),
            P(),
        ),
        out_specs=P("ctx", "head"),
        check_vma=False,
    )
```

```python
import jax
import jax.numpy as jnp
from jax import lax
from jax.experimental import pallas as pl
from jax.experimental.pallas import tpu as pltpu
from jax.sharding import PartitionSpec as P

MESH = pl.DeviceIdType.MESH
EPSILON = 1e-06
HD = 128
BLOCK = 128
RIM = 16
F32 = jnp.float32
BF16 = jnp.bfloat16
FAR = 1 << 20


def dot(a, b, dims=((1,), (0,))):
    return lax.dot_general(a, b, (dims, ((), ())), preferred_element_type=F32)


def halves(a):
    high = a.astype(BF16)
    return high, (a - high.astype(F32)).astype(BF16)


def dot3(a, b):
    width = b.shape[1]
    (a_high, a_low), (b_high, b_low) = halves(a), halves(b)
    left = jnp.concatenate([a_high, a_low], axis=1)
    right = jnp.concatenate(
        [jnp.concatenate([b_high, b_low], axis=1), jnp.concatenate([b_high, jnp.zeros_like(b_low)], axis=1)], axis=0
    )
    both = dot(left, right)
    return both[:, :width] + both[:, width:]


def dot2(a, b):
    width = b.shape[1]
    both = dot(a, jnp.concatenate(halves(b), axis=1))
    return both[:, :width] + both[:, width:]


def iota(shape, dim):
    return lax.broadcasted_iota(jnp.int32, shape, dim)


def each(function, *lists):
    return [function(*items) for items in zip(*lists)]


def unit_lower_inverses(lowers):
    size = lowers[0].shape[0]
    row, col = iota((size, size), 0), iota((size, size), 1)
    inverses = each(lambda lower: jnp.where(row == col, 1.0, 0.0), lowers)
    shift = 0
    while (1 << shift) < size:
        joins = ((row >> (shift + 1)) == (col >> (shift + 1))) & ((row >> shift) != (col >> shift))
        parts = each(lambda lower: jnp.where(joins, lower, 0.0), lowers)
        if shift > 0:
            parts = each(dot3, each(dot3, inverses, parts), inverses)
        inverses = each(lambda inverse, part: inverse - part, inverses, parts)
        shift += 1
    return inverses


def block_states(k, v, beta, g, start):
    row, col = iota((BLOCK, BLOCK), 0), iota((BLOCK, BLOCK), 1)
    lower_tri = row >= col
    ones = jnp.where(lower_tri, 1.0, 0.0).astype(BF16)
    gam = each(lambda g: dot2(ones, g), g)
    inner = each(lambda k: dot3(k, k.T), k)
    ratio, lead, lower = [], [], []
    for b in range(len(k)):
        same = lower_tri & (col >= start[b])
        ratio.append(jnp.where(same, jnp.exp(jnp.where(same, gam[b] - gam[b].T, 0.0)), 0.0))
        lead.append(jnp.where(start[b] < 0, jnp.exp(gam[b]), 0.0))
        lower.append(jnp.where(row > col, beta[b] * ratio[b] * inner[b], 0.0))
    rights, lasts = [], []
    for b in range(len(k)):
        rights.append(jnp.concatenate([beta[b] * v[b], beta[b] * lead[b] * k[b]], axis=1))
        tail = jnp.where(row >= start[b][BLOCK - 1 :], jnp.exp(gam[b][BLOCK - 1 :] - gam[b]), 0.0)
        lasts.append((tail * k[b]).T)
    inverses = unit_lower_inverses(lower)
    solved = each(dot3, inverses, rights)
    joint = each(dot3, lasts, solved)
    states = []
    for b in range(len(k)):
        transition = jnp.where(row == col, lead[b][BLOCK - 1 :], 0.0) - joint[b][:, HD:]
        states.append(jnp.concatenate([joint[b][:, :HD], transition], axis=1))
    return states, solved, ratio, lead


def compose(earlier, later):
    joined = dot3(later[:, HD:], earlier)
    return jnp.concatenate([joined[:, :HD] + later[:, :HD], joined[:, HD:]], axis=1)


def sigmoid(x):
    return 1.0 / (1.0 + jnp.exp(-x))


def kernel(
    tokens, w_query, w_key, w_value, w_gate, w_beta, w_decay, rate_in, bias_in, conv_qk_in, conv_value_in, gain_in, w_out,
    docs_in,
    out,
    quarter_stage, rim_stage, beta_w, rate, bias, conv_qk, conv_value, gain, docs,
    x_all, w_mine, w_other, wo_all, w_stage, piece, pieces, p_mine, p_other, acc, logit,
    z_unit, z_first, z_send, z_in, s_in, n_stage, n_all,
    send_sem, a1_sem, a2_sem, rim_sem, y_sem, p_sem, z_sem, c_sem, wo_sem, par_sem, zf_sem, zi_sem, si_sem, n_sem, own_sem,
    in_sem,
):
    ctx, head = lax.axis_index("ctx"), lax.axis_index("head")
    z, y = ctx // 8, ctx % 8
    x, c = head // 2, head % 2
    group, yl, yh = ctx // 4, ctx % 4, (ctx % 8) // 4
    hl = jnp.where(yh == 0, y, 7 - y)
    partner = (ctx, 2 * x + 1 - c)

    def place(g, local):
        g = lax.rem(g + 16, 16)
        return 8 * (g // 2) + jnp.where(g % 2 == 0, local, 7 - local)

    pending = []

    def send(src, dst, recv, device, cond=None):
        copy = pltpu.make_async_remote_copy(
            src_ref=src, dst_ref=dst, send_sem=send_sem.at[len(pending)], recv_sem=recv,
            device_id=device, device_id_type=MESH,
        )
        if cond is None:
            copy.start()
        else:
            pl.when(cond)(copy.start)
        pending.append((copy, cond))

    def sent(copy, cond):
        if cond is None:
            copy.wait_send()
        else:
            pl.when(cond)(copy.wait_send)

    def arrived(dst, sem):
        pltpu.make_async_copy(dst, dst, sem).wait()

    quarter = pl.ds(pl.multiple_of(32 * x, 32), 32)
    rim_lanes = pl.ds(pl.multiple_of(512 * x, 512), 512)

    inputs = [
        pltpu.make_async_copy(src, dst, in_sem.at[i])
        for i, (src, dst) in enumerate(
            [
                (w_query, w_stage.at[0, :, :HD]),
                (w_key, w_stage.at[0, :, HD:]),
                (w_value.at[:, :HD], w_stage.at[1, :, :HD]),
                (w_value.at[:, HD:], w_stage.at[2, :, :HD]),
                (w_gate.at[:, :HD], w_stage.at[1, :, HD:]),
                (w_gate.at[:, HD:], w_stage.at[2, :, HD:]),
                (w_beta, beta_w.at[0]),
                (w_decay, beta_w.at[1]),
                (rate_in, rate),
                (bias_in, bias),
                (conv_qk_in, conv_qk),
                (conv_value_in, conv_value),
                (gain_in, gain),
                (docs_in, docs),
                (tokens.at[quarter, :], quarter_stage),
                (tokens.at[pl.ds(128 - RIM, RIM), rim_lanes], rim_stage),
            ]
        )
    ]
    for copy in inputs[:8]:
        copy.start()

    barrier = pltpu.get_barrier_semaphore()

    def greet(device):
        pl.semaphore_signal(barrier, inc=1, device_id=device, device_id_type=MESH)

    for i in range(1, 8):
        other = 8 * z + lax.rem(y + i, 8)
        greet((other, 2 * x))
        greet((other, 2 * x + 1))
    for i in range(1, 8):
        greet((ctx, lax.rem(head + i, 8)))
    greet((lax.rem(ctx + 8, 64), head))
    greet((lax.rem(ctx + 56, 64), head))
    pl.when((c == 0) & (yh == 0))(lambda: greet((lax.rem(4 * group + 63, 64), 2 * x + 1)))

    @pl.when(c == 1)
    def _():
        for d in range(1, 5):
            greet((place(group - d, hl), head))

    rim_across = (c == 1) & (y == 7)

    for copy in inputs[8:]:
        copy.start()

    for copy in inputs[:8]:
        copy.wait()
    piece[...] = jnp.zeros((16, HD), BF16)
    for q in range(4):

        @pl.when(y % 4 == q)
        def _(q=q):
            piece[0:2, 32 * q : 32 * q + 32] = beta_w[0]
            piece[2:4, 32 * q : 32 * q + 32] = beta_w[1]

    pl.semaphore_wait(barrier, 23 + 4 * c + 4 * rim_across.astype(jnp.int32))

    mine_rows = pl.ds(pl.multiple_of(80 * (y // 2) + 32 * (y % 2), 16), 32)
    selfs = []
    for sub in range(2):
        local = 2 * c + sub
        for half in range(2):
            to = 8 * z + (local if half == 0 else 7 - local)
            me = to == ctx
            for core in range(2):
                device = (to, 2 * x + core)
                src = w_stage.at[0] if core == 0 else w_stage.at[1 + sub]
                is_self = me & (c == core)
                dst = w_mine.at[z, mine_rows, :]
                send(src, dst, y_sem.at[y], device, ~is_self)
                send(piece, pieces.at[y], p_sem.at[y], device, ~is_self)
                selfs.append((src, dst, is_self))
    for src, dst, is_self in selfs:

        @pl.when(is_self)
        def _(src=src, dst=dst):
            pltpu.make_async_copy(src, dst, y_sem.at[y]).start()
            pltpu.make_async_copy(piece, pieces.at[y], p_sem.at[y]).start()

    lanes = [pl.ds(1024 * i, 1024) for i in range(2)]

    def tokens_out():
        owner = yl // 2 == c
        rows = pl.ds(pl.multiple_of(RIM + 128 * (yl % 2) + 32 * x, 16), 32)
        for i in range(2):
            for j in range(1, 4):
                to = 4 * group + lax.rem(yl + j, 4)
                dst = x_all.at[rows, lanes[i]]
                send(quarter_stage.at[:, lanes[i]], dst, a1_sem.at[yl % 2, i], (to, head), owner)
        after_two = (c == 0) & (yl == 1)
        after_four = (c == 1) & (yl == 3)
        for j in range(4):
            to = jnp.where(after_two, 4 * group + j, lax.rem(4 * group + 4 + j, 64))
            dst = x_all.at[pl.ds(0, RIM), rim_lanes]
            send(rim_stage, dst, rim_sem.at[0], (to, 2 * x + 1 - c), after_two | after_four)

    for copy in inputs[8:]:
        copy.wait()
    for s in range(4):
        for i in range(2):
            p_mine[2 * s + i : 2 * s + i + 1, :] = conv_qk[s, i : i + 1, :]
        for i in range(2):
            p_mine[8 + 4 * i + s : 9 + 4 * i + s, :] = conv_value[s : s + 1, HD * i : HD * i + HD]
    for i in range(2):
        p_mine[16 + 2 * i : 17 + 2 * i, :] = jnp.full((1, HD), rate[i], F32)
        p_mine[17 + 2 * i : 18 + 2 * i, :] = jnp.full((1, HD), bias[i], F32)
    send(p_mine, p_other, par_sem, partner)
    own_block = []
    for k in range(2):
        is_own = yl == 2 * c + k
        block = x_all.at[pl.ds(RIM + 128 * k, 128), :]
        own_block.append((is_own, pltpu.make_async_copy(tokens, block, own_sem.at[0])))
        pl.when(is_own)(own_block[-1][1].start)
    own_out = pltpu.make_async_copy(
        w_out.at[:, pl.ds(pl.multiple_of(256 * head, 256), 256)],
        wo_all.at[pl.ds(pl.multiple_of(256 * head, 256), 256), :],
        own_sem.at[1],
    )
    own_out.start()

    base = 512 * group + 256 * c
    place_of = iota((256, HD), 0)
    start = jnp.full((256, HD), -FAR, jnp.int32)
    offset = -base
    for i in range(32):
        start = jnp.maximum(start, jnp.where(place_of >= offset, offset, -FAR))
        offset = offset + docs[i]

    ups, downs = lax.rem(ctx + 8, 64), lax.rem(ctx + 56, 64)
    parts = [lax.rem(y // 2 + i, 4) for i in (0, 1, 3, 2)]
    chunks = [pl.ds(pl.multiple_of(80 * part, 16), 64 if i < 3 else 80) for i, part in enumerate(parts)]
    narrow = [pl.ds(pl.multiple_of(80 * part, 16), 64) for part in parts]
    extra = pl.ds(pl.multiple_of(80 * parts[3] + 64, 16), 16)

    def onward(bundle, step, way, part):
        ref = w_mine.at[bundle, chunks[part], :]
        send(ref, ref, z_sem.at[way, step - 1, part], (ups if way == 0 else downs, head))

    def across(bundle, part):
        ref = narrow[part]
        send(w_mine.at[bundle, ref, :], w_other.at[bundle, ref, :], c_sem.at[bundle, part], partner)

    for part in range(4):
        for i in range(2):
            chip = 2 * parts[part] + i
            arrived(w_mine.at[z, pl.ds(pl.multiple_of(80 * parts[part] + 32 * i, 16), 32), :], y_sem.at[chip])
        if part == 3:
            for i in range(8):
                arrived(pieces.at[i], p_sem.at[i])
            for i in range(2):
                joined = sum(pieces[4 * i + j].astype(F32) for j in range(4))
                w_mine[z, extra, HD * i : HD * i + HD] = joined.astype(BF16)
        onward(z, 1, 0, part)
        onward(z, 1, 1, part)
        if part == 0:
            tokens_out()
        across(z, part)

    def tokens_on(i):
        for k in range(2):
            is_remote = yl != 2 * c + k
            rows = pl.ds(pl.multiple_of(RIM + 128 * k + 32 * x, 16), 32)
            ref = x_all.at[rows, lanes[i]]
            pl.when(is_remote)(lambda ref=ref, k=k: arrived(ref, a1_sem.at[k, i]))
            for j in (2, 1, 3):
                send(ref, ref, a2_sem.at[k, j - 1, i], (ctx, 2 * lax.rem(x + j, 4) + c), is_remote)

    def rim_on():
        ref = x_all.at[pl.ds(0, RIM), rim_lanes]
        arrived(ref, rim_sem.at[0])
        for j in (1, 3, 2):
            send(ref, ref, rim_sem.at[j], (ctx, 2 * lax.rem(x + j, 4) + c))

    def all_tokens():
        for k in range(2):

            @pl.when(yl != 2 * c + k)
            def _(k=k):
                for i in range(2):
                    for j in range(1, 4):
                        rows = pl.ds(pl.multiple_of(RIM + 128 * k + 32 * lax.rem(x + 4 - j, 4), 16), 32)
                        arrived(x_all.at[rows, lanes[i]], a2_sem.at[k, j - 1, i])

            pl.when(own_block[k][0])(own_block[k][1].wait)
        for j in range(1, 4):
            there = pl.ds(pl.multiple_of(512 * lax.rem(x + 4 - j, 4), 512), 512)
            arrived(x_all.at[pl.ds(0, RIM), there], rim_sem.at[j])

    def multiply(bundle, first):
        rows = x_all[:, pl.ds(pl.multiple_of(256 * bundle, 256), 256)]

        def add(which, weights):
            product = dot(rows, jnp.concatenate([weights[bundle, 80 * i : 80 * i + 64, :] for i in range(4)], axis=0))
            acc[which] = product if first else acc[which] + product

        add(c, w_mine)
        small = dot(rows, w_mine[bundle, extra, :], ((1,), (1,)))
        logit[...] = small if first else logit[...] + small
        for part in range(4):
            arrived(w_other.at[bundle, narrow[part], :], c_sem.at[bundle, part])
        add(1 - c, w_other)

    tokens_on(0)
    for step in range(1, 5):
        below, above = lax.rem(z + 8 - step, 8), lax.rem(z + step, 8)
        for part in range(4):
            for way, bundle in ((0, below), (1, above)):
                if step == 4 and part // 2 != way:
                    continue
                arrived(w_mine.at[bundle, chunks[part], :], z_sem.at[way, step - 1, part])
                if step < 3 or (step == 3 and part // 2 == way):
                    onward(bundle, step + 1, way, part)
                across(bundle, part)
        if step == 1:
            tokens_on(1)
        if step == 1:
            rim_on()
        if step == 3:
            all_tokens()
            multiply(z, True)
            for near in range(1, 3):
                multiply(lax.rem(z + 8 - near, 8), False)
                multiply(lax.rem(z + near, 8), False)
    for i in range(1, 8):
        to = lax.rem(head + i, 8)
        src = w_out.at[:, pl.ds(pl.multiple_of(256 * to, 256), 256)]
        dst = wo_all.at[pl.ds(pl.multiple_of(256 * head, 256), 256), :]
        send(src, dst, wo_sem.at[i - 1], (ctx, to))

    for near in range(3, 5):
        multiply(lax.rem(z + 8 - near, 8), False)
        if near < 4:
            multiply(lax.rem(z + near, 8), False)

    arrived(p_other, par_sem)
    settings = jnp.where(hl // 2 == c, p_mine[...], p_other[...])
    second = hl % 2 == 1
    acc[...] = acc[...].astype(BF16).astype(F32)

    def convolved(side, lanes, taps):
        total = acc[side, RIM : RIM + 256, lanes] * taps[3]
        for s in range(3):
            shifted = acc[side, RIM - 3 + s : RIM - 3 + s + 256, lanes]
            total = total + jnp.where(place_of - 3 + s >= start, shifted, 0.0) * taps[s]
        return total * sigmoid(total)

    def pick(low, high):
        return jnp.where(second, settings[high : high + 1], settings[low : low + 1])

    q_act = convolved(0, slice(0, HD), [settings[2 * s : 2 * s + 1] for s in range(4)])
    k_act = convolved(0, slice(HD, 2 * HD), [settings[2 * s + 1 : 2 * s + 2] for s in range(4)])
    v_act = convolved(1, slice(0, HD), [pick(8 + s, 12 + s) for s in range(4)])
    q_act = q_act * (lax.rsqrt(jnp.sum(q_act * q_act, axis=1, keepdims=True) + EPSILON) * HD**-0.5)
    k_act = k_act * lax.rsqrt(jnp.sum(k_act * k_act, axis=1, keepdims=True) + EPSILON)
    logits = logit[RIM:, :]
    beta_logit = jnp.where(second, logits[:, 1:2], logits[:, 0:1])
    decay_logit = jnp.where(second, logits[:, 3:4], logits[:, 2:3])
    beta = jnp.broadcast_to(sigmoid(beta_logit), (256, HD))
    shifted = jnp.broadcast_to(decay_logit, (256, HD)) + pick(17, 19)
    softplus = jnp.maximum(shifted, 0.0) + jnp.log1p(jnp.exp(-jnp.abs(shifted)))
    decay = -pick(16, 18) * softplus

    def blocks(array):
        return [array[:BLOCK], array[BLOCK:]]

    q_two, k_two, start_two = blocks(q_act), blocks(k_act), blocks(start)
    states, solved, ratio, lead = block_states(
        k_two, blocks(v_act), blocks(beta), blocks(decay), [start_two[0], start_two[1] - BLOCK]
    )
    z_unit[...] = compose(states[0], states[1])
    send(z_unit, z_first, zf_sem, partner, c == 0)

    targets = [(place(group + d, hl), head) for d in range(1, 5)]
    size = [2 * HD, 2 * HD, 2 * HD, HD]

    @pl.when(c == 1)
    def _():
        arrived(z_first, zf_sem)
        z_send[...] = compose(z_first[...], z_unit[...]).astype(BF16)

    for d in (2, 3, 0, 1):
        part = pl.ds(0, size[d])
        send(z_send.at[:, part], z_in.at[d, :, part], zi_sem.at[d], targets[d], c == 1)

    scores = each(lambda q, k, ratio: dot3(q, k.T) * ratio, q_two, k_two, ratio)
    mixed = each(dot3, scores, solved)
    leads = each(lambda q, lead, mixed: lead * q - mixed[:, HD:], q_two, lead, mixed)
    rests = each(lambda mixed: mixed[:, :HD], mixed)
    through = dot3(leads[1], states[0])
    leads[1], rests[1] = through[:, HD:], rests[1] + through[:, :HD]
    gate = acc[1, RIM:, HD:]
    gate = gate * sigmoid(gate) * gain[...]
    done = len(pending) - 5
    for copy, cond in pending[:done]:
        sent(copy, cond)

    @pl.when(c == 1)
    def _():
        for d in range(4):
            arrived(z_in.at[d, :, pl.ds(0, size[d])], zi_sem.at[d])
        state = z_in[3, :, :HD].astype(F32)
        for d in (2, 1, 0):
            state = dot2(z_in[d, :, HD:], state) + z_in[d, :, :HD].astype(F32)
        s_in[0] = state

    send(s_in.at[0], s_in.at[1], si_sem, partner, c == 1)
    pl.when(c == 0)(lambda: arrived(s_in.at[1], si_sem))

    @pl.when(c == 1)
    def _():
        s_in[1] = dot3(z_first[:, HD:], s_in[0]) + z_first[:, :HD]

    before = s_in[1]
    my_head = 4 * x + hl
    for b in range(2):
        rows = slice(BLOCK * b, BLOCK * b + BLOCK)
        result = dot3(leads[b], before) + rests[b]
        scale = lax.rsqrt(jnp.mean(result * result, axis=1, keepdims=True) + EPSILON)
        n_stage[rows, :] = (result * scale * gate[rows]).astype(BF16)
        src = n_stage.at[pl.ds(BLOCK * b, BLOCK), :]
        dst = n_all.at[my_head]
        is_self = (yl == 2 * c + b) & (hl % 2 == c)
        device = (4 * group + 2 * c + b, 2 * x + hl % 2)
        send(src, dst, n_sem.at[my_head], device, ~is_self)
        pl.when(is_self)(lambda src=src, dst=dst: pltpu.make_async_copy(src, dst, n_sem.at[my_head]).start())
    for m in range(2):
        which = 4 * x + 2 * m + c
        ref = n_all.at[which]
        arrived(ref, n_sem.at[which])
        for i in (1, 3, 2):
            send(ref, ref, n_sem.at[which], (ctx, 2 * lax.rem(x + i, 4) + c))
        send(ref, ref, n_sem.at[which], partner)
    for i in (1, 3, 2):
        for m in range(2):
            which = 4 * lax.rem(x + i, 4) + 2 * m + c
            ref = n_all.at[which]
            arrived(ref, n_sem.at[which])
            send(ref, ref, n_sem.at[which], partner)
    for i in range(1, 8):
        rows = pl.ds(pl.multiple_of(256 * lax.rem(head + 8 - i, 8), 256), 256)
        arrived(wo_all.at[rows, :], wo_sem.at[i - 1])
    own_out.wait()
    total = jnp.zeros((128, 256), F32)
    for core in (c, 1 - c):
        for i in range(4):
            pair = [4 * i + core, 4 * i + 2 + core]
            for which in pair:
                if core is not c:
                    arrived(n_all.at[which], n_sem.at[which])
            rows = jnp.concatenate([n_all[which] for which in pair], axis=1)
            weights = [wo_all[pl.ds(pl.multiple_of(128 * which, 128), 128), :] for which in pair]
            total = total + dot(rows, jnp.concatenate(weights, axis=0))
    out[...] = total.astype(BF16)

    for copy, cond in pending[done:]:
        sent(copy, cond)


def local(
    tokens, w_query, w_key, w_value, w_output_gate, w_beta, w_decay, decay_rate, dt_bias, conv_qk, conv_value, norm_gain,
    w_out, doc_lengths,
):
    vmem = pl.BlockSpec(memory_space=pltpu.VMEM)
    dma = pltpu.SemaphoreType.DMA
    return pl.pallas_call(
        kernel,
        out_shape=pltpu.VMEM((128, 256), BF16),
        in_specs=[pl.BlockSpec(memory_space=pltpu.HBM)] * 14,
        out_specs=vmem,
        scratch_shapes=[
            pltpu.VMEM((32, 2048), BF16),
            pltpu.VMEM((RIM, 512), BF16),
            pltpu.VMEM((2, 2, 32), BF16),
            pltpu.SMEM((2,), F32),
            pltpu.SMEM((2,), F32),
            pltpu.VMEM((4, 2, HD), F32),
            pltpu.VMEM((4, 256), F32),
            pltpu.VMEM((1, HD), F32),
            pltpu.SMEM((32,), jnp.int32),
            pltpu.VMEM((RIM + 256, 2048), BF16),
            pltpu.VMEM((8, 320, 256), BF16),
            pltpu.VMEM((8, 320, 256), BF16),
            pltpu.VMEM((2048, 256), BF16),
            pltpu.VMEM((3, 32, 256), BF16),
            pltpu.VMEM((16, HD), BF16),
            pltpu.VMEM((8, 16, HD), BF16),
            pltpu.VMEM((24, HD), F32),
            pltpu.VMEM((24, HD), F32),
            pltpu.VMEM((2, RIM + 256, 256), F32),
            pltpu.VMEM((RIM + 256, 16), F32),
            pltpu.VMEM((HD, 2 * HD), F32),
            pltpu.VMEM((HD, 2 * HD), F32),
            pltpu.VMEM((HD, 2 * HD), BF16),
            pltpu.VMEM((4, HD, 2 * HD), BF16),
            pltpu.VMEM((2, HD, HD), F32),
            pltpu.VMEM((256, HD), BF16),
            pltpu.VMEM((16, 128, HD), BF16),
            dma((144,)),
            dma((2, 2)),
            dma((2, 3, 2)),
            dma((4,)),
            dma((8,)),
            dma((8,)),
            dma((2, 4, 4)),
            dma((8, 4)),
            dma((7,)),
            dma,
            dma,
            dma((4,)),
            dma,
            dma((16,)),
            dma((2,)),
            dma((16,)),
        ],
        compiler_params=pltpu.CompilerParams(
            collective_id=0, has_side_effects=True, vmem_limit_bytes=60 * 2**20
        ),
    )(
        tokens, w_query, w_key, w_value, w_output_gate, w_beta.T, w_decay.T, decay_rate, dt_bias, conv_qk, conv_value,
        norm_gain.reshape(1, HD), w_out, doc_lengths,
    )


def solution(mesh):
    return jax.shard_map(
        local,
        mesh=mesh,
        in_specs=(
            P("ctx", None),
            P("ctx", "head"),
            P("ctx", "head"),
            P("ctx", "head"),
            P("ctx", "head"),
            P("ctx", "head"),
            P("ctx", "head"),
            P("head"),
            P("head"),
            P(None, None, "head"),
            P(None, "head"),
            P(),
            P("head", None),
            P(),
        ),
        out_specs=P("ctx", "head"),
        check_vma=False,
    )
```
